32 devices in a mesh: dp: 8 (over z, x), head: 4 (over y, core).
Axes of the slice: x: 2, y: 2, z: 4, core: 2. Of those that a mesh axis runs over, the one named last changes fastest.
Arguments:
- tokens: bfloat16 [64, 512, 768], P('dp', 'head'), may hold values from -6 to 6
- bucket_of_block: int32 [8, 8], P('dp'), may hold values from 0 to 2, as said below
- lengths: int32 [8, 8, 4], P('dp'), may hold values from 0 to 512, as said below
- w_query: bfloat16 [768, 768], replicated, may hold values from -0.109375 to 0.109375
- w_key: bfloat16 [768, 768], replicated, may hold values from -0.109375 to 0.109375
- w_value: bfloat16 [768, 768], replicated, may hold values from -0.21875 to 0.21875
- w_out: bfloat16 [768, 768], replicated, may hold values from -0.625 to 0.625
- w_in: bfloat16 [768, 3072], replicated, may hold values from -0.21875 to 0.21875
- w_back: bfloat16 [3072, 768], replicated, may hold values from -0.109375 to 0.109375
- gain_attn: float32 [768], replicated, may hold values from 0.5 to 1.5
- gain_ffn: float32 [768], replicated, may hold values from 0.5 to 1.5
- bias_table: float32 [32, 12], P(None, 'head'), may hold values from -4 to 4
- cotangent: bfloat16 [64, 512, 768], P('dp', 'head'), may hold values from -6 to 6
Outputs:
- output: bfloat16 [64, 512, 768], P('dp', 'head')
- grad_tokens: bfloat16 [64, 512, 768], P('dp', 'head')
- grad_w_query: float32 [768, 768], P('dp', 'head')
- grad_w_key: float32 [768, 768], P('dp', 'head')
- grad_w_value: float32 [768, 768], P('dp', 'head')
- grad_w_out: float32 [768, 768], P('dp', 'head')
- grad_w_in: float32 [768, 3072], P('dp', 'head')
- grad_w_back: float32 [3072, 768], P('dp', 'head')
- grad_gain_attn: float32 [768], P('head')
- grad_gain_ffn: float32 [768], P('head')
- grad_bias_table: float32 [32, 12], P(None, 'head')
The draws below stay inside these ranges and needn't reach their ends.
Inputs may be any that keep to these rules, and one draw needn't show every extreme that they name: A block with bucket b holds 4 // 2**b documents of 512 // 4 * 2**b slots each; every row of bucket_of_block has one or more blocks with b = 2. `lengths`: entry s of a block is the real length of its document s for s < 4 // 2**b, between a quarter of the document's slots and all of them, and 0 for the other entries; every row has a block of bucket 2 that holds one document of exactly 512 tokens.
All inputs are finite; a program needn't handle non-finite values.
Results may differ from the reference program's by a relative error of at most 0.015.
Values may be sent and summed in bfloat16 or wider, within the bound.
A program may use at most 192 MiB of HBM per device.

```python
import math
import jax
import jax.numpy as jnp
from jax import lax

D = 768
HEADS = 12
HEAD_DIM = 64
FF = 3072
BUCKETS = 32
BLOCK = 512
BLK_DEV = 8
PACKS = 8
SEQBLK = 64


def shared_layout(key):
    keys = jax.random.split(key, 3)
    per_group = BLK_DEV
    bucket_ids = jax.random.randint(keys[0], (PACKS, per_group), 0, 3)
    forced = jax.random.randint(keys[1], (PACKS, 1), 0, per_group)
    columns = jnp.arange(per_group)[None, :]
    chosen = (columns == forced).reshape(SEQBLK)
    bucket_ids = jnp.where(columns == forced, 2, bucket_ids).reshape(SEQBLK).astype(jnp.int32)
    span = BLOCK // 4 * jnp.where(bucket_ids == 0, 1, jnp.where(bucket_ids == 1, 2, 4))
    lowest = span // 4
    drawn = jax.random.randint(keys[2], (SEQBLK, 4), lowest[:, None], span[:, None] + 1)
    slots = jnp.arange(4)[None, :]
    drawn = jnp.where(slots < (BLOCK // span)[:, None], drawn, 0)
    first_slot = jnp.where(chosen, BLOCK, drawn[:, 0])
    drawn = jnp.concatenate([first_slot[:, None], drawn[:, 1:]], axis=1)
    return (bucket_ids.reshape(PACKS, BLK_DEV), drawn.astype(jnp.int32).reshape(PACKS, BLK_DEV, 4))


def draw_bucket_of_block(key, part):
    shared = shared_layout(key)
    return shared[0]


def draw_lengths(key, part):
    shared = shared_layout(key)
    return shared[1]


def block_levels(rng, shape, cuts, low, high):
    loudness, own = 1.0, jax.random.fold_in(rng, 6)
    for axis_at, shards_of in cuts:
        draws = jnp.exp(jax.random.uniform(jax.random.fold_in(own, axis_at), (shards_of,), jnp.float32, low / len(cuts), high / len(cuts)))
        loudness = loudness * jnp.repeat(draws, shape[axis_at] // shards_of).reshape([-1 if axis == axis_at else 1 for axis in range(len(shape))])
    return loudness


def noise(key, dims, deviation, limit, cuts=(), kind=jnp.bfloat16):
    values = jax.random.normal(key, dims, jnp.float32) * deviation
    if len(cuts) > 0:
        values = block_levels(key, dims, cuts, -0.22, 0.18) * values
    return jnp.clip(values, min=-limit, max=limit).astype(kind)


def setup_inputs(seed: int = 0) -> dict:
    streams_of = jax.random.split(jax.random.key(seed), 14)
    tokens = noise(streams_of[0], (SEQBLK, BLOCK, D), 1.0, 6.0, ((0, 8), (1, 4)))
    bucket_of_block = draw_bucket_of_block(jax.random.fold_in(streams_of[13], 71), 0)
    lengths = draw_lengths(jax.random.fold_in(streams_of[13], 71), 0)
    w_query = noise(streams_of[3], (D, D), (4 * D) ** -0.5, 0.109375)
    w_key = noise(streams_of[4], (D, D), (4 * D) ** -0.5, 0.109375)
    w_value = noise(streams_of[5], (D, D), D ** -0.5, 0.21875)
    w_out = noise(streams_of[6], (D, D), (D // 8) ** -0.5, 0.625)
    w_in = noise(streams_of[7], (D, FF), D ** -0.5, 0.21875)
    w_back = noise(streams_of[8], (FF, D), FF ** -0.5, 0.109375)
    gain_attn = jnp.clip(1.0 + 0.1 * jax.random.normal(streams_of[9], (D,), jnp.float32), 0.5, 1.5)
    gain_ffn = jnp.clip(1.0 + 0.1 * jax.random.normal(streams_of[10], (D,), jnp.float32), 0.5, 1.5)
    bias_table = noise(streams_of[11], (BUCKETS, HEADS), 1.0, 4.0, ((1, 4),), jnp.float32)
    cotangent = noise(streams_of[12], (SEQBLK, BLOCK, D), 1.0, 6.0, ((0, 8), (1, 4)))
    return dict(tokens=tokens, bucket_of_block=bucket_of_block, lengths=lengths, w_query=w_query, w_key=w_key, w_value=w_value, w_out=w_out, w_in=w_in, w_back=w_back, gain_attn=gain_attn, gain_ffn=gain_ffn, bias_table=bias_table, cotangent=cotangent)


@jax.custom_vjp
def low(v):
    return lax.optimization_barrier(v.astype(jnp.bfloat16)).astype(jnp.float32)

@jax.custom_vjp
def low_back(v):
    return v

def low_keep(v):
    return (low(v), None)

def low_pass(kept, grad):
    return (grad,)

def back_keep(v):
    return (v, None)

def back_low(kept, grad):
    return (low(grad),)
low.defvjp(low_keep, low_pass)
low_back.defvjp(back_keep, back_low)
EPSILON = 1e-06

def matmul_high(left, right):
    return jnp.dot(left, right, precision=lax.Precision.HIGHEST)

def rms_norm(values, gain):
    return values * lax.rsqrt(lax.optimization_barrier(jnp.mean(values * values, axis=-1, keepdims=True)) + EPSILON) * gain

def smooth_act(values):
    return jax.nn.gelu(values, approximate=True)

def rel_bucket(offset):
    direction_part = jnp.where(offset > 0, 16, 0).astype(jnp.int32)
    magnitude = jnp.abs(offset).astype(jnp.int32)
    far_bucket = jnp.full_like(magnitude, 8)
    for threshold in (12, 16, 23, 32, 46, 64, 91):
        far_bucket = far_bucket + (magnitude >= threshold).astype(jnp.int32)
    return direction_part + jnp.where(magnitude < 8, magnitude, far_bucket)

def block_masks(bucket_ids, seq_lengths):
    positions = jnp.arange(BLOCK, dtype=jnp.int32)
    span = BLOCK // 4 * jnp.where(bucket_ids == 0, 1, jnp.where(bucket_ids == 1, 2, 4)).astype(jnp.int32)
    sequence = positions[None, :] // span[:, None]
    within = positions[None, :] % span[:, None]
    slots = jnp.arange(4, dtype=jnp.int32)
    key_length = lax.optimization_barrier(jnp.sum(jnp.where(sequence[:, :, None] == slots, seq_lengths[:, None, :], 0), axis=-1))
    live_key = within < key_length
    return (sequence[:, :, None] == sequence[:, None, :]) & live_key[:, None, :]

def encoder_layer(inputs, weights, valid_pairs, onehot):
    w_query, w_key, w_value, w_out, w_in, w_back, gain_attn, gain_ffn, bias_table = weights
    groups = inputs.shape[0]
    flat_rows = inputs.reshape(groups * BLOCK, D)
    normed_attn = low(rms_norm(flat_rows, gain_attn))

    def heads_of(weight):
        projected = low_back(low(matmul_high(normed_attn, weight)))
        return projected.reshape(groups, BLOCK, HEADS, HEAD_DIM)
    queries_all = heads_of(w_query)
    keys_all = heads_of(w_key)
    values_all = heads_of(w_value)
    raw_scores = jnp.einsum('gqhd,gkhd->ghqk', queries_all, keys_all, precision=lax.Precision.HIGHEST)
    position_bias = jnp.einsum('qkb,bh->hqk', onehot, bias_table, precision=lax.Precision.HIGHEST)
    scores = jnp.where(valid_pairs[:, None], low_back(raw_scores) + position_bias[None], -1000000000.0)
    probabilities = jax.nn.softmax(scores, axis=-1)
    context = jnp.einsum('ghqk,gkhd->gqhd', low(probabilities), values_all, precision=lax.Precision.HIGHEST)
    context = low_back(low(context)).reshape(groups * BLOCK, D)
    hidden = flat_rows + low_back(matmul_high(context, w_out))
    normed_ffn = low(rms_norm(hidden, gain_ffn))
    activated = low(smooth_act(low_back(matmul_high(normed_ffn, w_in))))
    return (hidden + matmul_high(activated, w_back)).reshape(groups, BLOCK, D)

def reference(tokens, bucket_of_block, lengths, w_query, w_key, w_value, w_out, w_in, w_back, gain_attn, gain_ffn, bias_table, cotangent):
    params = (w_query.astype(jnp.float32), w_key.astype(jnp.float32), w_value.astype(jnp.float32), w_out.astype(jnp.float32), w_in.astype(jnp.float32), w_back.astype(jnp.float32), gain_attn.astype(jnp.float32), gain_ffn.astype(jnp.float32), bias_table.astype(jnp.float32))
    group_size = math.gcd(SEQBLK, 8)
    step_count = SEQBLK // group_size
    positions = jnp.arange(BLOCK, dtype=jnp.int32)
    offsets = (positions[None, :] - positions[:, None]).astype(jnp.int32)
    onehot = (rel_bucket(offsets)[:, :, None] == jnp.arange(BUCKETS, dtype=jnp.int32)).astype(jnp.float32)

    def one_step(sums, inputs):
        token_group, bucket_group, length_group, grad_group = inputs
        valid_pairs = block_masks(bucket_group, length_group)

        def forward(token_values, *weights):
            return encoder_layer(token_values, weights, valid_pairs, onehot)
        result, pullback = jax.vjp(forward, token_group.astype(jnp.float32), *params)
        grads = pullback(grad_group.astype(jnp.float32))
        new_sums = tuple((total + part_grad for total, part_grad in zip(sums, grads[1:])))
        return (new_sums, (result.astype(jnp.bfloat16), grads[0].astype(jnp.bfloat16)))
    stacked = (tokens.reshape(step_count, group_size, BLOCK, D), bucket_of_block.reshape(step_count, group_size), lengths.reshape(step_count, group_size, 4), cotangent.reshape(step_count, group_size, BLOCK, D))
    zeros = tuple((jnp.zeros_like(param) for param in params))
    sums, (result_all, grad_all) = lax.scan(one_step, zeros, stacked)
    return (result_all.reshape(SEQBLK, BLOCK, D), grad_all.reshape(SEQBLK, BLOCK, D), sums[0], sums[1], sums[2], sums[3], sums[4], sums[5], sums[6], sums[7], sums[8])
```

```python
import functools
import math

import jax
import jax.numpy as jnp
from jax import lax
from jax.experimental import pallas as pl
from jax.experimental.pallas import tpu as pltpu
from jax.sharding import PartitionSpec as P

D = 768
HEADS = 12
FF = 3072
BUCKETS = 32
BLOCK = 512
PAIRS = 6
OWN = 2
GROUP = 4
ROWS = 8
EPSILON = 1e-06
TILE = 128
MASKED = -1000000000.0
GELU_A = math.sqrt(2.0 / math.pi)
GELU_B = 0.044715

bf16 = jnp.bfloat16
f32 = jnp.float32
MESH = pl.DeviceIdType.MESH
ANY = pl.BlockSpec(memory_space=pl.ANY)
VMEM = pl.BlockSpec(memory_space=pltpu.VMEM)
SMEM = pl.BlockSpec(memory_space=pltpu.SMEM)
DMA = pltpu.SemaphoreType.DMA
STEPS = 3


def nn(left, right):
    return jnp.dot(left, right, preferred_element_type=f32)


def nt(left, right):
    return lax.dot_general(left, right, (((1,), (1,)), ((), ())), preferred_element_type=f32)


def tn(left, right):
    return lax.dot_general(left, right, (((0,), (0,)), ((), ())), preferred_element_type=f32)


def flat(ref, lanes=slice(None)):
    value = ref[:, :, lanes]
    return value.reshape(value.shape[0] * value.shape[1], value.shape[2])


def head_masks():
    lane = lax.broadcasted_iota(jnp.int32, (1, TILE), 1)
    low = (lane < TILE // 2).astype(f32)
    return low.astype(bf16), (1.0 - low).astype(bf16)


def bucket_of(offset):
    magnitude = jnp.abs(offset)
    far = jnp.full(offset.shape, 8, jnp.int32)
    for threshold in (12, 16, 23, 32, 46, 64, 91):
        far = far + (magnitude >= threshold).astype(jnp.int32)
    side = jnp.where(offset > 0, 16, 0).astype(jnp.int32)
    return side + jnp.where(magnitude < 8, magnitude, far)


def skew_offsets(tile):
    lane = lax.broadcasted_iota(jnp.int32, (1, 2 * TILE), 1)
    return TILE * tile + jnp.where(lane < TILE, -lane, 2 * TILE - lane)


def attend_kernel(
    tokens, cot, table, w_q, w_k, w_v, gain, buckets, lengths,
    x_out, cot_out, n_out, q_out, k_out, v_out, ctx_out, p_out,
    xs, ns, qs, ks, vs, cs, ps, wq, wk, wv, tabs, tiles, mask,
    own_sem, send_sem, recv_sem, cot_own, cot_send, cot_recv, tab_send, tab_recv, w_sem, out_sem, p_sem,
):
    me = lax.axis_index("head")
    y, c = me // 2, me % 2
    peers = ((1 - y) * 2 + c, (1 - y) * 2 + (1 - c), y * 2 + (1 - c))
    barrier = pltpu.get_barrier_semaphore()
    for peer in peers:
        pl.semaphore_signal(barrier, inc=1, device_id={"head": peer}, device_id_type=MESH)

    def mine(start):
        return pl.ds(pl.multiple_of(start * TILE, TILE), TILE)

    locals_ = []
    for blk in range(OWN):
        copy = pltpu.make_async_copy(tokens.at[me + GROUP * blk], xs.at[blk, mine(me)], own_sem.at[blk])
        copy.start()
        locals_.append(copy)
    weights = []
    for at, (src, dst) in enumerate(((w_q, wq), (w_k, wk), (w_v, wv))):
        copy = pltpu.make_async_copy(src, dst, w_sem.at[at])
        copy.start()
        weights.append(copy)
    own_cot = []
    for blk in range(OWN):
        copy = pltpu.make_async_copy(cot.at[me + GROUP * blk], cot_out.at[blk, mine(me)], cot_own.at[blk])
        copy.start()
        own_cot.append(copy)

    tabs[me] = table[...]
    pl.semaphore_wait(barrier, len(peers))

    def send(source, dest, sends, recvs, blk, at):
        return pltpu.make_async_remote_copy(
            src_ref=source.at[peers[at] + GROUP * blk],
            dst_ref=dest.at[blk, mine(me)],
            send_sem=sends.at[blk, at],
            recv_sem=recvs.at[blk, at],
            device_id={"head": peers[at]},
            device_id_type=MESH,
        )

    moves = [[send(tokens, xs, send_sem, recv_sem, blk, at) for at in range(3)] for blk in range(OWN)]
    cot_moves = [[send(cot, cot_out, cot_send, cot_recv, blk, at) for at in range(3)] for blk in range(OWN)]
    tab_moves = [
        pltpu.make_async_remote_copy(
            src_ref=table,
            dst_ref=tabs.at[me],
            send_sem=tab_send.at[at],
            recv_sem=tab_recv.at[at],
            device_id={"head": peers[at]},
            device_id_type=MESH,
        )
        for at in range(3)
    ]
    for at in range(3):
        moves[0][at].start()
    for at in range(3):
        tab_moves[at].start()
    for at in range(3):
        moves[1][at].start()

    key = lax.broadcasted_iota(jnp.int32, (BLOCK, BLOCK), 0)
    query = lax.broadcasted_iota(jnp.int32, (1, BLOCK), 1)
    for blk in range(OWN):
        block = me + GROUP * blk
        bucket = buckets[0, block]
        span = TILE * jnp.where(bucket == 0, 1, jnp.where(bucket == 1, 2, 4))
        start = jnp.zeros((1, BLOCK), jnp.int32)
        end = jnp.zeros((1, BLOCK), jnp.int32)
        for slot in range(4):
            inside = query >= slot * span
            start = jnp.where(inside, slot * span, start)
            end = jnp.where(inside, slot * span + lengths[0, block, slot], end)
        mask[blk] = jnp.where((key >= start) & (key < end), 0.0, MASKED).astype(f32)

    for copy in tab_moves:
        copy.wait()
    bucket_rows = [bucket_of(skew_offsets(tile)) for tile in (-1, 0, 1)]
    for group in range(GROUP):
        rows = tabs[group]
        for tile in range(3):
            values = jnp.zeros((8, 2 * TILE), f32)
            for bucket in range(BUCKETS):
                values = jnp.where(bucket_rows[tile] == bucket, rows[:, bucket : bucket + 1], values)
            for at in range(3):
                wide = jnp.broadcast_to(values[at : at + 1], (TILE, 2 * TILE))
                wide = pltpu.roll(wide, 0, 1, stride=1, stride_axis=0)
                tiles[3 * group + at, 1 + tile] = wide[:, :TILE]
        for at in range(3):
            tiles[3 * group + at, 0] = jnp.broadcast_to(rows[at : at + 1, 15:16], (TILE, TILE))
            tiles[3 * group + at, 4] = jnp.broadcast_to(rows[at : at + 1, 31:32], (TILE, TILE))

    def project(blk, half):
        rows = pl.ds(pl.multiple_of(half * 256, 256), 256)
        x = xs[blk, rows, :].astype(f32)
        r = lax.rsqrt(jnp.mean(x * x, axis=-1, keepdims=True) + EPSILON)
        normed = (x * r * gain[...]).astype(bf16)
        ns[blk, rows, :] = normed
        qs[blk, rows, :] = nn(normed, wq[...]).astype(bf16)
        ks[blk, rows, :] = nn(normed, wk[...]).astype(bf16)
        vs[blk, rows, :] = nn(normed, wv[...]).astype(bf16)

    for copy in weights:
        copy.wait()
    for blk in range(OWN):
        locals_[blk].wait()
        moves[blk][2].wait()
        project(blk, y)

    low, high = head_masks()
    drains = []

    def drain(src, dst, at):
        copy = pltpu.make_async_copy(src, dst, out_sem.at[at])
        copy.start()
        drains.append(copy)

    for blk in range(OWN):
        moves[blk][0].wait()
        moves[blk][1].wait()
        for copy in cot_moves[blk]:
            copy.start()
        project(blk, 1 - y)
        for at, (src, dst) in enumerate(((xs, x_out), (ns, n_out), (qs, q_out), (ks, k_out), (vs, v_out))):
            drain(src.at[blk], dst.at[blk], 5 * blk + at)

        def attend(pair, carry):
            lanes = pl.ds(pl.multiple_of(pair * TILE, TILE), TILE)
            q, k, v = qs[blk, :, lanes], ks[blk, :, lanes], vs[blk, :, lanes]
            slot = blk * PAIRS + pair
            total = None
            for e, sel in enumerate((low, high)):
                scores = nt(k, q * sel)
                head = 2 * pair + e
                for qt in range(4):
                    at_q = slice(TILE * qt, TILE * qt + TILE)
                    parts = []
                    for kt in range(4):
                        at_k = slice(TILE * kt, TILE * kt + TILE)
                        kind = min(max(kt - qt, -2), 2) + 2
                        parts.append(scores[at_k, at_q] + tiles[head, kind] + mask[blk, at_k, at_q])
                    peak = parts[0]
                    for part in parts[1:]:
                        peak = jnp.maximum(peak, part)
                    peak = jnp.max(peak, axis=0, keepdims=True)
                    parts = [jnp.exp(part - peak) for part in parts]
                    whole = parts[0] + parts[1] + parts[2] + parts[3]
                    scale = 1.0 / jnp.sum(whole, axis=0, keepdims=True)
                    for kt in range(4):
                        ps[slot, e, TILE * kt : TILE * kt + TILE, at_q] = (parts[kt] * scale).astype(bf16)
                part = tn(ps[slot, e], v * sel)
                total = part if total is None else total + part
            cs[blk, :, lanes] = total.astype(bf16)
            pltpu.make_async_copy(ps.at[slot], p_out.at[slot], p_sem.at[slot]).start()
            return carry

        lax.fori_loop(0, PAIRS, attend, 0)
        drain(cs.at[blk], ctx_out.at[blk], 10 + blk)

    for slot in range(OWN * PAIRS):
        pltpu.make_async_copy(ps.at[slot], p_out.at[slot], p_sem.at[slot]).wait()
    for copy in drains:
        copy.wait()
    for blk in range(OWN):
        own_cot[blk].wait()
        for copy in cot_moves[blk]:
            copy.wait()


def attend_call(tokens, cot, table, w_q, w_k, w_v, gain, buckets, lengths):
    rows = jax.ShapeDtypeStruct((OWN, BLOCK, D), bf16)
    probs = jax.ShapeDtypeStruct((OWN * PAIRS, 2, BLOCK, BLOCK), bf16)
    block_rows = pltpu.VMEM((OWN, BLOCK, D), bf16)
    square = pltpu.VMEM((D, D), bf16)
    return pl.pallas_call(
        attend_kernel,
        out_shape=(rows,) * 7 + (probs,),
        in_specs=[ANY, ANY, VMEM, ANY, ANY, ANY, VMEM, SMEM, SMEM],
        out_specs=(ANY,) * 8,
        scratch_shapes=[block_rows] * 6
        + [pltpu.VMEM(probs.shape, bf16), square, square, square]
        + [
            pltpu.VMEM((GROUP, 8, TILE), f32),
            pltpu.VMEM((HEADS, 5, TILE, TILE), f32),
            pltpu.VMEM((OWN, BLOCK, BLOCK), f32),
            DMA((OWN,)), DMA((OWN, 3)), DMA((OWN, 3)),
            DMA((OWN,)), DMA((OWN, 3)), DMA((OWN, 3)),
            DMA((3,)), DMA((3,)), DMA((3,)), DMA((12,)), DMA((OWN * PAIRS,)),
        ],
        compiler_params=pltpu.CompilerParams(collective_id=0, has_side_effects=True, vmem_limit_bytes=60 * 2**20),
    )(tokens, cot, table, w_q, w_k, w_v, gain, buckets, lengths)


AXES = ("x", "z0", "y", "z1")
ORDERS = (("x", "y", "z0", "z1"), ("z0", "x", "y", "z1"))
UNIT = (2, 2, 2, 2, 96, TILE)


def rest_kernel(
    outer,
    x_in, cot_in, n_in, q_in, k_in, v_in, ctx_in, p_in, w_q, w_k, w_v, w_o, w_in, w_back, gain_a, gain_f,
    output, grad_tokens, g_qkvo, g_in, g_back, g_small,
    xs, cots, ns, cs, hidden, total, back, dcs, wo, own,
    c_ffn, c_att, r0_ffn, r1_ffn, r2_ffn, r3_ffn, r0_att, r1_att, r2_att, r3_att,
    f_ffn, f_att, rf_ffn, rf_att, small, small_in, buckets_acc,
    in_sem, cs_send, cs_recv, ca_send, ca_recv, st_send, st_recv, fx_send, fx_recv, sm_send, sm_recv,
    out_own, out_send, out_recv,
):
    me = lax.axis_index("head")
    dp = lax.axis_index("dp")
    y, c = me // 2, me % 2
    chunk, spare = dp // outer, dp % outer
    z1, z0, x = chunk // 4, (chunk // 2) % 2, chunk % 2
    place = {"x": x, "y": y, "z0": z0, "z1": z1}

    def device(row, column):
        return {"dp": row * outer + spare, "head": column}

    partner = {
        "c": device(chunk, 2 * y + (1 - c)),
        "y": device(chunk, 2 * (1 - y) + c),
        "x": device(chunk + 1 - 2 * x, me),
        "z0": device(chunk + 2 - 4 * z0, me),
        "z1": device(chunk + 4 - 8 * z1, me),
    }
    peers = ((1 - y) * 2 + c, (1 - y) * 2 + (1 - c), y * 2 + (1 - c))
    greeted = [partner[axis] for axis in ("c", "y", "x", "z0", "z1")] + [{"head": peers[1]}]
    barrier = pltpu.get_barrier_semaphore()
    for other in greeted:
        pl.semaphore_signal(barrier, inc=1, device_id=other, device_id_type=MESH)

    loads = []
    for at, (src, dst) in enumerate(((ctx_in, cs), (w_o, wo), (x_in, xs), (cot_in, cots), (n_in, ns))):
        copy = pltpu.make_async_copy(src, dst, in_sem.at[at])
        copy.start()
        loads.append(copy)

    pl.semaphore_wait(barrier, len(greeted))

    def remote(src, dst, sends, recvs, other):
        return pltpu.make_async_remote_copy(
            src_ref=src, dst_ref=dst, send_sem=sends, recv_sem=recvs, device_id=other, device_id_type=MESH
        )

    def ffn_base(item, kind):
        return (item * 2 + kind) * 4

    def core_copies(item):
        if item < STEPS:
            copies = [
                remote(own.at[pl.ds(ffn_base(item, 1 - c), 4)], c_ffn.at[item], cs_send.at[item], cs_recv.at[item], partner["c"])
            ]
        else:
            g = item - STEPS
            copies = [
                remote(
                    own.at[ffn_base(g, 1 - c) + 2 * half + (1 - c)], c_att.at[g, half],
                    ca_send.at[g, half], ca_recv.at[g, half], partner["c"],
                )
                for half in range(2)
            ]
        return copies

    def add_into(target, arrived):
        target[...] = target[...] + arrived[...]

    def core_finish(item):
        for copy in core_copies(item):
            copy.wait()
        if item < STEPS:
            base = ffn_base(item, c)

            def add(at, carry):
                for b in range(2):
                    add_into(own.at[base + at, b], c_ffn.at[item, at, b])
                return carry

            lax.fori_loop(0, 4, add, 0)
        else:
            g = item - STEPS
            for half in range(2):
                slot = ffn_base(g, 1 - c) + 2 * half + c

                def add(b, carry):
                    add_into(own.at[slot, b], c_att.at[g, half, b])
                    return carry

                lax.fori_loop(0, 2, add, 0)

    def part(item, half, done, axis=None, value=None):
        index = []
        for name in ("z1", "z0", "x", "y"):
            if name == axis:
                index.append(value)
            elif name in done:
                index.append(place[name])
            else:
                index.append(slice(None))
        if item < STEPS:
            lead = pl.ds(ffn_base(item, c) + 2 * half, 2)
        else:
            lead = ffn_base(item - STEPS, 1 - c) + 2 * half + c
        return own.at[tuple([lead] + index)]

    stage_ffn = (r0_ffn, r1_ffn, r2_ffn, r3_ffn)
    stage_att = (r0_att, r1_att, r2_att, r3_att)

    def arrived_at(item, half, stage):
        if item < STEPS:
            return stage_ffn[stage].at[item, half]
        return stage_att[stage].at[item - STEPS, half]

    def stage_copies(item, stage):
        copies = []
        for half in range(2):
            order = ORDERS[half]
            axis = order[stage]
            copy = remote(
                part(item, half, order[:stage], axis, 1 - place[axis]), arrived_at(item, half, stage),
                st_send.at[item, half, stage], st_recv.at[item, half, stage], partner[axis],
            )
            copies.append(copy)
        return copies

    def stage_finish(item, stage):
        copies = stage_copies(item, stage)
        for half in range(2):
            copies[half].wait()
            order = ORDERS[half]
            kept = part(item, half, order[: stage + 1])
            arrived = arrived_at(item, half, stage)
            if stage < 3:
                add_into(kept, arrived)
            elif item < STEPS:
                f_ffn[item, half] = kept[...] + arrived[...]
            else:
                f_att[item - STEPS, half] = kept[...] + arrived[...]

    def fix_copies(item):
        if item < STEPS:
            copy = remote(f_ffn.at[item, 1 - c], rf_ffn.at[item], fx_send.at[item], fx_recv.at[item], partner["c"])
        else:
            g = item - STEPS
            copy = remote(f_att.at[g], rf_att.at[g], fx_send.at[item], fx_recv.at[item], partner["c"])
        return [copy]

    state = {}

    def advance(item):
        at = state.get(item, 0)
        state[item] = min(at + 1, 7)
        if at == 1:
            core_finish(item)
        elif 2 <= at < 6:
            stage_finish(item, at - 2)
        if at == 0:
            copies = core_copies(item)
        elif at < 5:
            copies = stage_copies(item, at - 1)
        elif at < 7:
            copies = fix_copies(item)
        else:
            copies = []
        for copy in copies:
            if at == 6:
                copy.wait()
            else:
                copy.start()

    for copy in loads[:3]:
        copy.wait()

    def project_out(at, carry):
        blk, half = at // 2, at % 2
        rows = pl.ds(pl.multiple_of(half * 256, 256), 256)
        hidden[blk, rows, :] = xs[blk, rows, :].astype(f32) + nn(cs[blk, rows, :], wo[...])
        return carry

    lax.fori_loop(0, 4, project_out, 0)

    def feed_forward(nf, act, dinner, win, wback, w_sem):
        def fetch(step):
            slot = step % 2
            copies = []
            for f in range(8):
                at = f * (FF // 8) + step * TILE
                into = pl.ds(f * TILE, TILE)
                copies.append(pltpu.make_async_copy(w_in.at[:, pl.ds(at, TILE)], win.at[slot, :, into], w_sem.at[slot, 0, f]))
                copies.append(pltpu.make_async_copy(w_back.at[pl.ds(at, TILE)], wback.at[slot, into], w_sem.at[slot, 1, f]))
            for copy in copies:
                copy.start()
            return copies

        fetched = [fetch(0), fetch(1)]

        def norm(at, carry):
            blk, half = at // 2, at % 2
            rows = pl.ds(pl.multiple_of(half * 256, 256), 256)
            h = hidden[blk, rows, :]
            r = lax.rsqrt(jnp.mean(h * h, axis=-1, keepdims=True) + EPSILON)
            nf[blk, rows, :] = (h * r * gain_f[...]).astype(bf16)
            return carry

        lax.fori_loop(0, 4, norm, 0)
        loads[3].wait()

        for step in range(STEPS):
            slot = step % 2
            for copy in fetched[step]:
                copy.wait()

            def rows_of(at, carry):
                blk, half = at // 2, at % 2
                rows = pl.ds(pl.multiple_of(half * 256, 256), 256)
                v = nn(nf[blk, rows, :], win[slot])
                square = v * v
                t = jnp.tanh(GELU_A * v * (1.0 + GELU_B * square))
                a = (0.5 * v * (1.0 + t)).astype(bf16)
                slope = 0.5 * (1.0 + t) + 0.5 * GELU_A * v * (1.0 - t * t) * (1.0 + 3.0 * GELU_B * square)
                act[blk, rows, :] = a
                g = (nt(cots[blk, rows, :], wback[slot]) * slope).astype(bf16)
                dinner[blk, rows, :] = g
                onward = nn(a, wback[slot])
                backward = nt(g, win[slot])
                if step == 0:
                    total[blk, rows, :] = hidden[blk, rows, :] + onward
                    back[blk, rows, :] = backward
                else:
                    total[blk, rows, :] += onward
                    back[blk, rows, :] += backward
                return carry

            lax.fori_loop(0, 4, rows_of, 0)
            if step >= 1:
                advance(step - 1)
            if step >= 2:
                advance(step - 2)
            if step + 2 < STEPS:
                fetched.append(fetch(step + 2))
            for b in range(2):
                res = tn(flat(nf), flat(dinner, slice(512 * b, 512 * b + 512))).astype(bf16)
                for m in range(4):
                    own[ffn_base(step, 0) + m, :, :, :, b] = res[:, TILE * m : TILE * m + TILE].reshape(2, 2, 2, 96, TILE)
            for b in range(2):
                res = tn(flat(cots, slice(384 * b, 384 * b + 384)), flat(act)).astype(bf16)
                for m in range(4):
                    for f in range(8):
                        own[ffn_base(step, 1) + m, f // 4, (f // 2) % 2, f % 2, b] = res[
                            96 * m : 96 * m + 96, TILE * f : TILE * f + TILE
                        ]
            advance(step)

    pl.run_scoped(
        feed_forward,
        nf=pltpu.VMEM((OWN, BLOCK, D), bf16),
        act=pltpu.VMEM((OWN, BLOCK, 1024), bf16),
        dinner=pltpu.VMEM((OWN, BLOCK, 1024), bf16),
        win=pltpu.VMEM((2, D, 1024), bf16),
        wback=pltpu.VMEM((2, 1024, D), bf16),
        w_sem=DMA((2, 2, 8)),
    )

    def send_back(rows_of, result, at_blk, sems_at):
        copies = []
        for at in range(3):
            copies.append(
                remote(
                    rows_of.at[at_blk, pl.ds(pl.multiple_of(peers[at] * TILE, TILE), TILE)],
                    result.at[me + GROUP * at_blk],
                    out_send.at[sems_at, at_blk, at], out_recv.at[sems_at, at_blk, at], {"head": peers[at]},
                )
            )
        copies.append(
            pltpu.make_async_copy(
                rows_of.at[at_blk, pl.ds(pl.multiple_of(me * TILE, TILE), TILE)],
                result.at[me + GROUP * at_blk], out_own.at[sems_at, at_blk],
            )
        )
        return copies

    def start_back(rows_of, result, at_blk, sems_at):
        for copy in send_back(rows_of, result, at_blk, sems_at):
            copy.start()

    def wait_back(rows_of, result, sems_at):
        for blk in range(OWN):
            for copy in send_back(rows_of, result, blk, sems_at):
                copy.wait()

    small[0] = jnp.zeros((32, TILE), f32)
    buckets_acc[...] = jnp.zeros_like(buckets_acc)

    def attention(qs, ks, vs, ps, dsb, acc, wq, wk, wv, l_sem, p_sem):
        more = []
        for at, (src, dst) in enumerate(((q_in, qs), (k_in, ks), (v_in, vs), (w_q, wq), (w_k, wk), (w_v, wv))):
            copy = pltpu.make_async_copy(src, dst, l_sem.at[at])
            copy.start()
            more.append(copy)

        def index_of(n):
            group, within = n // 4, n % 4
            return (within % 2) * PAIRS + group + 3 * (within // 2)

        def probs_copy(n):
            return pltpu.make_async_copy(p_in.at[index_of(n)], ps.at[n % 2], p_sem.at[n % 2])

        probs_copy(0).start()

        def close(at, gains):
            blk, half = at // 2, at % 2
            rows = pl.ds(pl.multiple_of(half * 256, 256), 256)
            h = hidden[blk, rows, :]
            r = lax.rsqrt(jnp.mean(h * h, axis=-1, keepdims=True) + EPSILON)
            d = back[blk, rows, :]
            scaled = gain_f[...] * d
            inner = jnp.mean(h * scaled, axis=-1, keepdims=True)
            grad = cots[blk, rows, :].astype(f32) + r * scaled - h * (r * r * r * inner)
            cots[blk, rows, :] = total[blk, rows, :].astype(bf16)
            hidden[blk, rows, :] = grad
            low_grad = grad.astype(bf16)
            dcs[blk, rows, :] = nt(low_grad, wo[...]).astype(bf16)
            return gains + jnp.sum(d * h * r, axis=0, keepdims=True)

        gains = lax.fori_loop(0, 4, close, jnp.zeros((1, D), f32))
        for m in range(6):
            small[0, 22 + m : 23 + m, :] = gains[:, TILE * m : TILE * m + TILE]
        for blk in range(OWN):
            start_back(cots, output, blk, 0)
        advance(1)
        advance(0)
        for copy in more:
            copy.wait()
        loads[4].wait()

        low, high = head_masks()
        corner = lax.broadcasted_iota(jnp.int32, (TILE, TILE), 0) + lax.broadcasted_iota(jnp.int32, (TILE, TILE), 1)
        flip = (corner == TILE - 1).astype(f32)
        for group in range(3):
            for side in range(2):
                pair = group + 3 * side
                lanes = slice(TILE * pair, TILE * pair + TILE)
                acc[...] = jnp.zeros_like(acc)

                def one(blk, carry):
                    n = 4 * group + 2 * side + blk
                    slot = n % 2
                    probs_copy(n).wait()

                    @pl.when(n + 1 < OWN * PAIRS)
                    def _():
                        probs_copy(n + 1).start()

                    q, k, v, dc = qs[blk, :, lanes], ks[blk, :, lanes], vs[blk, :, lanes], dcs[blk, :, lanes]
                    dq = dk = dv = None
                    for e, sel in enumerate((low, high)):
                        dce = dc * sel
                        grads = nt(v, dce)
                        for qt in range(4):
                            at_q = slice(TILE * qt, TILE * qt + TILE)
                            probs = [ps[slot, e, TILE * kt : TILE * kt + TILE, at_q].astype(f32) for kt in range(4)]
                            parts = [probs[kt] * grads[TILE * kt : TILE * kt + TILE, at_q] for kt in range(4)]
                            delta = jnp.sum(parts[0] + parts[1] + parts[2] + parts[3], axis=0, keepdims=True)
                            for kt in range(4):
                                ds = parts[kt] - probs[kt] * delta
                                acc[e, min(max(kt - qt, -2), 2) + 2] += ds
                                dsb[e, TILE * kt : TILE * kt + TILE, at_q] = ds.astype(bf16)
                        terms = (tn(dsb[e], k * sel), nn(dsb[e], q * sel), nn(ps[slot, e], dce))
                        if e == 0:
                            dq, dk, dv = terms
                        else:
                            dq, dk, dv = dq + terms[0], dk + terms[1], dv + terms[2]
                    qs[blk, :, lanes] = dq.astype(bf16)
                    ks[blk, :, lanes] = dk.astype(bf16)
                    vs[blk, :, lanes] = dv.astype(bf16)
                    return carry

                lax.fori_loop(0, OWN, one, 0)
                for e in range(2):
                    sums = []
                    for tile in range(3):
                        turned = jnp.dot(flip, acc[e, 1 + tile], preferred_element_type=f32, precision=lax.Precision.HIGHEST)
                        wide = jnp.concatenate([turned, jnp.zeros((TILE, TILE), f32)], axis=1)
                        wide = pltpu.roll(wide, 0, 1, stride=1, stride_axis=0)
                        sums.append(jnp.sum(wide, axis=0, keepdims=True))
                    buckets_acc[2 * pair + e : 2 * pair + e + 1, 0:768] = jnp.concatenate(sums, axis=1)
                    buckets_acc[2 * pair + e : 2 * pair + e + 1, 768:896] = jnp.sum(acc[e, 0], axis=0, keepdims=True)
                    buckets_acc[2 * pair + e : 2 * pair + e + 1, 896:1024] = jnp.sum(acc[e, 4], axis=0, keepdims=True)
                if side == 0:
                    if group == 0:
                        advance(2), advance(1), advance(0)
                    elif group == 1:
                        advance(2), advance(1), advance(0), advance(3)
                    else:
                        advance(2), advance(1), advance(4), advance(3)
            for side in range(2):
                pair = group + 3 * side
                lanes = slice(TILE * pair, TILE * pair + TILE)
                qk = tn(flat(ns), jnp.concatenate([flat(t, lanes) for t in (qs, ks)], axis=1)).astype(bf16)
                grad_v = tn(flat(ns), flat(vs, lanes)).astype(bf16)
                grad_o = tn(flat(cs), flat(hidden, lanes).astype(bf16)).astype(bf16)
                pieces = ((qk[:, :TILE], qk[:, TILE:]), (grad_v, grad_o))
                base = ffn_base(group, 1 - c)
                for kind in range(2):
                    for half in range(2):
                        own[base + 2 * half + kind, :, :, :, side] = pieces[kind][half].reshape(2, 2, 2, 96, TILE)
            item = STEPS + group
            advance(item)
            if group == 0:
                advance(2), advance(1), advance(0)
            elif group == 1:
                advance(2), advance(3), advance(1), advance(0)
            else:
                advance(5), advance(4), advance(3), advance(2)


        def first_norm(at, gains):
            blk, half = at // 2, at % 2
            rows = pl.ds(pl.multiple_of(half * 256, 256), 256)
            d = nt(qs[blk, rows, :], wq[...]) + nt(ks[blk, rows, :], wk[...]) + nt(vs[blk, rows, :], wv[...])
            h = xs[blk, rows, :].astype(f32)
            r = lax.rsqrt(jnp.mean(h * h, axis=-1, keepdims=True) + EPSILON)
            scaled = gain_a[...] * d
            inner = jnp.mean(h * scaled, axis=-1, keepdims=True)
            xs[blk, rows, :] = (hidden[blk, rows, :] + r * scaled - h * (r * r * r * inner)).astype(bf16)
            return gains + jnp.sum(d * h * r, axis=0, keepdims=True)

        gains = lax.fori_loop(0, 2, first_norm, jnp.zeros((1, D), f32))
        start_back(xs, grad_tokens, 0, 1)
        advance(5), advance(4), advance(3)
        gains = lax.fori_loop(2, 4, first_norm, gains)
        start_back(xs, grad_tokens, 1, 1)
        for m in range(6):
            small[0, 16 + m : 17 + m, :] = gains[:, TILE * m : TILE * m + TILE]

    pl.run_scoped(
        attention,
        qs=pltpu.VMEM((OWN, BLOCK, D), bf16),
        ks=pltpu.VMEM((OWN, BLOCK, D), bf16),
        vs=pltpu.VMEM((OWN, BLOCK, D), bf16),
        ps=pltpu.VMEM((2, 2, BLOCK, BLOCK), bf16),
        dsb=pltpu.VMEM((2, BLOCK, BLOCK), bf16),
        acc=pltpu.VMEM((2, 5, TILE, TILE), f32),
        wq=pltpu.VMEM((D, D), bf16),
        wk=pltpu.VMEM((D, D), bf16),
        wv=pltpu.VMEM((D, D), bf16),
        l_sem=DMA((6,)),
        p_sem=DMA((2,)),
    )

    lane = lax.broadcasted_iota(jnp.int32, (1, 2 * TILE), 1)
    offsets = jnp.concatenate([TILE * tile + TILE - 1 - lane for tile in (-1, 0, 1)], axis=1)
    far = lax.broadcasted_iota(jnp.int32, (1, 256), 1)
    column = jnp.concatenate([bucket_of(offsets), jnp.where(far < TILE, 15, 31)], axis=1)
    hot = (lax.broadcasted_iota(jnp.int32, (TILE, 1024), 0) == column).astype(f32)
    small[0, 0:16, :] = lax.dot_general(
        buckets_acc[...], hot, (((1,), (1,)), ((), ())), preferred_element_type=f32, precision=lax.Precision.HIGHEST
    )
    for at, axis in enumerate(("c", "y", "x", "z0", "z1")):
        copy = remote(small.at[at], small_in.at[at], sm_send.at[at], sm_recv.at[at], partner[axis])
        copy.start()
        if at < 4:
            for item in range(6):
                if state[item] < 7:
                    advance(item)
        copy.wait()
        if at < 4:
            small[at + 1] = small[at] + small_in[at]
        else:
            g_small[...] = small[at] + small_in[at]
    while any(state[item] < 7 for item in range(6)):
        for item in range(6):
            if state[item] < 7:
                advance(item)
    wait_back(cots, output, 0)
    wait_back(xs, grad_tokens, 1)
    emit(c, f_ffn, rf_ffn, f_att, rf_att, g_qkvo, g_in, g_back)


def emit(c, f_ffn, rf_ffn, f_att, rf_att, g_qkvo, g_in, g_back):
    first = c == 0
    for step in range(STEPS):
        for b in range(2):
            kept, got = f_ffn[step, c, b].astype(f32), rf_ffn[step, b].astype(f32)
            g_in[:, 384 * b + TILE * step : 384 * b + TILE * step + TILE] = jnp.where(first, kept, got)
            g_back[TILE * step : TILE * step + TILE, 96 * b : 96 * b + 96] = jnp.where(first, got, kept).T
    for half in range(2):
        for kind in range(2):
            pieces = []
            for g in range(3):
                kept, got = f_att[g, half].astype(f32), rf_att[g, half].astype(f32)
                pieces.append(jnp.where(first, kept, got) if kind == 0 else jnp.where(first, got, kept))
            wide = jnp.concatenate(pieces, axis=1)
            at = 2 * kind + half
            g_qkvo[at] = jnp.where(first, wide[:, :192], wide[:, 192:])


def rest_call(outer, x, cot, n, q, k, v, ctx, probs, w_q, w_k, w_v, w_o, w_in, w_back, gain_a, gain_f):
    rows = (OWN, BLOCK, D)
    local = jax.ShapeDtypeStruct((ROWS, TILE, D), bf16)
    halves = (3, 2)
    scratch = [
        pltpu.VMEM(rows, bf16),
        pltpu.VMEM(rows, bf16),
        pltpu.VMEM(rows, bf16),
        pltpu.VMEM(rows, bf16),
        pltpu.VMEM(rows, f32),
        pltpu.VMEM(rows, f32),
        pltpu.VMEM(rows, f32),
        pltpu.VMEM(rows, bf16),
        pltpu.VMEM((D, D), bf16),
        pltpu.VMEM((24,) + UNIT, bf16),
        pltpu.VMEM((3, 4) + UNIT, bf16),
        pltpu.VMEM((3, 2) + UNIT, bf16),
    ]
    for dims in ((2,), ()):
        for stage in range(4):
            scratch.append(pltpu.VMEM(halves + dims + (2,) * (3 - stage) + UNIT[4:], bf16))
    scratch += [
        pltpu.VMEM((3, 2, 2) + UNIT[4:], bf16),
        pltpu.VMEM((3, 2) + UNIT[4:], bf16),
        pltpu.VMEM((3, 2) + UNIT[4:], bf16),
        pltpu.VMEM((3, 2) + UNIT[4:], bf16),
        pltpu.VMEM((5, 32, TILE), f32),
        pltpu.VMEM((5, 32, TILE), f32),
        pltpu.VMEM((16, 1024), f32),
        DMA((5,)), DMA((3,)), DMA((3,)), DMA((3, 2)), DMA((3, 2)),
        DMA((6, 2, 4)), DMA((6, 2, 4)), DMA((6,)), DMA((6,)), DMA((5,)), DMA((5,)),
        DMA((2, OWN)), DMA((2, OWN, 3)), DMA((2, OWN, 3)),
    ]
    return pl.pallas_call(
        functools.partial(rest_kernel, outer),
        out_shape=(
            local,
            local,
            jax.ShapeDtypeStruct((4, 96, 192), f32),
            jax.ShapeDtypeStruct((96, D), f32),
            jax.ShapeDtypeStruct((384, 192), f32),
            jax.ShapeDtypeStruct((32, TILE), f32),
        ),
        in_specs=[ANY] * 14 + [VMEM, VMEM],
        out_specs=(ANY, ANY, VMEM, VMEM, VMEM, VMEM),
        scratch_shapes=scratch,
        compiler_params=pltpu.CompilerParams(collective_id=1, has_side_effects=True, vmem_limit_bytes=63 * 2**20),
    )(x, cot, n, q, k, v, ctx, probs, w_q, w_k, w_v, w_o, w_in, w_back, gain_a, gain_f)


def shards(
    tokens, bucket_of_block, lengths, w_query, w_key, w_value, w_out, w_in, w_back, gain_attn, gain_ffn, bias_table, cotangent
):
    devices = lax.axis_size("dp")
    outer = devices // 8
    gain_a, gain_f = gain_attn.reshape(1, D), gain_ffn.reshape(1, D)
    per = bias_table.shape[1]
    table = jnp.pad(bias_table.T, ((0, 8 - per), (0, TILE - BUCKETS)))
    kept = attend_call(tokens, cotangent, table, w_query, w_key, w_value, gain_a, bucket_of_block, lengths)
    output, grad_tokens, g_qkvo, g_in, g_back, g_small = rest_call(
        outer, *kept, w_query, w_key, w_value, w_out, w_in, w_back, gain_a, gain_f
    )
    weights = [g_qkvo[0], g_qkvo[1], g_qkvo[2], g_qkvo[3], g_in, g_back]
    if outer > 1:
        groups = [[at * outer + spare for spare in range(outer)] for at in range(8)]
        weights = [
            lax.psum_scatter(grad, "dp", scatter_dimension=0, axis_index_groups=groups, tiled=True) for grad in weights
        ]
        g_small = lax.psum(g_small, "dp", axis_index_groups=groups)
    me = lax.axis_index("head")
    gains = g_small[16:28].reshape(2, D)
    gains = lax.dynamic_slice(gains, (0, me * (D // GROUP)), (2, D // GROUP))
    table_grad = lax.dynamic_slice(g_small, (me * per, 0), (per, BUCKETS)).T
    return (output, grad_tokens, *weights, gains[0], gains[1], table_grad)


def solution(mesh):
    whole = P()
    rows = P("dp", "head", None)
    block = P("dp", "head")
    return jax.shard_map(
        shards,
        mesh=mesh,
        in_specs=(rows, P("dp", None), P("dp", None, None)) + (whole,) * 8 + (P(None, "head"), rows),
        out_specs=(rows, rows) + (block,) * 6 + (P("head"), P("head"), P(None, "head")),
        check_vma=False,
    )
```

```python
import functools
import math

import jax
import jax.numpy as jnp
from jax import lax
from jax.experimental import pallas as pl
from jax.experimental.pallas import tpu as pltpu
from jax.sharding import PartitionSpec as P

D = 768
HEADS = 12
FF = 3072
BUCKETS = 32
BLOCK = 512
PAIRS = 6
OWN = 2
GROUP = 4
ROWS = 8
EPSILON = 1e-06
TILE = 128
MASKED = -float(2**30)
GELU_A = math.sqrt(2.0 / math.pi)
GELU_B = 0.044715

bf16 = jnp.bfloat16
f32 = jnp.float32
MESH = pl.DeviceIdType.MESH
ANY = pl.BlockSpec(memory_space=pl.ANY)
VMEM = pl.BlockSpec(memory_space=pltpu.VMEM)
DMA = pltpu.SemaphoreType.DMA
STEPS = 3


def nn(left, right):
    return jnp.dot(left, right, preferred_element_type=f32)


def nt(left, right):
    return lax.dot_general(left, right, (((1,), (1,)), ((), ())), preferred_element_type=f32)


def tn(left, right):
    return lax.dot_general(left, right, (((0,), (0,)), ((), ())), preferred_element_type=f32)


def flat(ref, lanes=slice(None)):
    value = ref[:, :, lanes]
    return value.reshape(value.shape[0] * value.shape[1], value.shape[2])


def head_masks():
    lane = lax.broadcasted_iota(jnp.int32, (1, TILE), 1)
    low = (lane < TILE // 2).astype(f32)
    return low.astype(bf16), (1.0 - low).astype(bf16)


def bucket_of(offset):
    magnitude = jnp.abs(offset)
    far = jnp.full(offset.shape, 8, jnp.int32)
    for threshold in (12, 16, 23, 32, 46, 64, 91):
        far = far + (magnitude >= threshold).astype(jnp.int32)
    side = jnp.where(offset > 0, 16, 0).astype(jnp.int32)
    return side + jnp.where(magnitude < 8, magnitude, far)


def skew_offsets(tile):
    lane = lax.broadcasted_iota(jnp.int32, (1, 2 * TILE), 1)
    return TILE * tile + jnp.where(lane < TILE, -lane, 2 * TILE - lane)


ORDERS = (
    (("x", "z0", "z1", "y"), ("z0", "x", "y", "z1")),
    (("x", "z0", "z1", "y"), ("z0", "x", "y", "z1")),
    (("x", "z0", "z1", "y"), ("z0", "x", "y", "z1")),
    (("x", "z0", "z1", "y"), ("z0", "x", "y", "z1")),
    (("x", "z0", "z1", "y"), ("z0", "x", "y", "z1")),
    (("x", "z0", "z1", "y"), ("z0", "x", "y", "z1")),
)
UNIT = (2, 2, 2, 2, 96, TILE)
SLOTS = 4

PLAN = {
    "ffn0": [(0, 1)],
    "rows1.3": [(0, 2)],
    "ffn1": [(1, 1)],
    "rows2.3": [(0, 3), (1, 2)],
    "ffn2": [(2, 1)],
    "close.1": [(0, 4)],
    "closed": [("out", 0)],
    "first.1": [("out", 1), (2, 2)],
    "first.2": [("out", 2)],
    "first.3": [("out", 3)],
    "first.4": [("out", 4), (1, 3)],
    "first.5": [("out", 5)],
    "norm0.0": [(0, 5)],
    "side0": [(2, 3)],
    "group0": [(3, 1)],
    "second1.1": [(1, 4)],
    "second1.2": [(3, 2), (0, 6)],
    "group1": [(0, 7), (2, 4), (4, 1)],
    "side2": [(4, 2)],
    "group2": [(1, 5), (3, 3), (5, 1)],
    "small0": [(2, 5), (4, 3), (5, 2)],
    "small1": [(1, 6), (3, 4)],
    "last": [(1, 7), (4, 4), (2, 6), (2, 7), (5, 3), (3, 5), (4, 5), (5, 4), (3, 6), (4, 6), (3, 7), (4, 7), (5, 5), (5, 6), (5, 7)],
}


def layer_kernel(
    outer,
    tokens, cot, table, buckets, lengths, w_q, w_k, w_v, w_o, w_in, w_back, gain_a, gain_f,
    output, grad_tokens, g_q, g_k, g_v, g_o, g_in, g_back, g_small, q_kept, k_kept, v_kept, p_kept,
    xs, cots, ns, cs, hidden, total, back, dcs, wo, invs, tab, tabs, own,
    c_ffn, c_att, r0_ffn, r1_ffn, r2_ffn, r3_ffn, r0_att, r1_att, r2_att, r3_att,
    f_ffn, f_att, rf_ffn, rf_att, small, small_in, small_far, buckets_acc,
    own_sem, send_sem, recv_sem, cot_own, cot_send, cot_recv, tab_send, tab_recv, wo_sem,
    cs_send, cs_recv, ca_send, ca_recv, st_send, st_recv, fx_send, fx_recv, sm_send, sm_recv,
    out_own, out_send, out_recv,
):
    me = lax.axis_index("head")
    dp = lax.axis_index("dp")
    y, c = me // 2, me % 2
    chunk, spare = dp // outer, dp % outer
    z1, z0, x = chunk // 4, (chunk // 2) % 2, chunk % 2
    place = {"x": x, "y": y, "z0": z0, "z1": z1}

    def device(row, column):
        return {"dp": row * outer + spare, "head": column}

    partner = {
        "c": device(chunk, 2 * y + (1 - c)),
        "y": device(chunk, 2 * (1 - y) + c),
        "x": device(chunk + 1 - 2 * x, me),
        "z0": device(chunk + 2 - 4 * z0, me),
        "z1": device(chunk + 4 - 8 * z1, me),
    }
    peers = ((1 - y) * 2 + c, (1 - y) * 2 + (1 - c), y * 2 + (1 - c))
    column_peers = [device((chunk + at) % 8, me) for at in range(1, 8)]
    greeted = [{"head": peer} for peer in peers] + column_peers
    barrier = pltpu.get_barrier_semaphore()
    for other in greeted:
        pl.semaphore_signal(barrier, inc=1, device_id=other, device_id_type=MESH)

    def remote(src, dst, sends, recvs, other):
        return pltpu.make_async_remote_copy(
            src_ref=src, dst_ref=dst, send_sem=sends, recv_sem=recvs, device_id=other, device_id_type=MESH
        )

    def mine(start):
        return pl.ds(pl.multiple_of(start * TILE, TILE), TILE)

    x_own = [pltpu.make_async_copy(tokens.at[me + GROUP * blk], xs.at[blk, mine(me)], own_sem.at[blk]) for blk in range(OWN)]
    c_own = [pltpu.make_async_copy(cot.at[me + GROUP * blk], cots.at[blk, mine(me)], cot_own.at[blk]) for blk in range(OWN)]
    wo_copy = pltpu.make_async_copy(w_o, wo, wo_sem)
    for copy in x_own:
        copy.start()
    tab[...] = jnp.zeros_like(tab)
    tab[0 : table.shape[0], 0:BUCKETS] = table[...]
    tabs[me] = tab[...]
    pl.semaphore_wait(barrier, len(greeted))

    def send(source, dest, sends, recvs, blk, at):
        return remote(
            source.at[peers[at] + GROUP * blk], dest.at[blk, mine(me)], sends.at[blk, at], recvs.at[blk, at], {"head": peers[at]}
        )

    moves = [[send(tokens, xs, send_sem, recv_sem, blk, at) for at in range(3)] for blk in range(OWN)]
    cot_moves = [[send(cot, cots, cot_send, cot_recv, blk, at) for at in range(3)] for blk in range(OWN)]
    tab_moves = [remote(tab, tabs.at[me], tab_send.at[at], tab_recv.at[at], {"head": peers[at]}) for at in range(3)]
    for copy in tab_moves:
        copy.start()
    for blk in range(OWN):
        for copy in moves[blk]:
            copy.start()

    low, high = head_masks()

    def attention(qs, ks, vs, ps, wq, wk, wv, tiles, marks, w_sem, keep_sem, p_sem):
        weights = [
            pltpu.make_async_copy(src, dst, w_sem.at[at])
            for at, (src, dst) in enumerate(((w_q, wq), (w_k, wk), (w_v, wv)))
        ]
        for copy in weights:
            copy.start()
        for copy in c_own:
            copy.start()
        wo_copy.start()

        def project(blk, half):
            rows = pl.ds(pl.multiple_of(half * 256, 256), 256)
            x = xs[blk, rows, :].astype(f32)
            r = lax.rsqrt(jnp.mean(x * x, axis=-1, keepdims=True) + EPSILON)
            normed = (x * r * gain_a[...].reshape(1, D)).astype(bf16)
            ns[blk, rows, :] = normed
            qs[blk, rows, :] = nn(normed, wq[...]).astype(bf16)
            ks[blk, rows, :] = nn(normed, wk[...]).astype(bf16)
            vs[blk, rows, :] = nn(normed, wv[...]).astype(bf16)

        row = lax.broadcasted_iota(jnp.int32, (BLOCK, TILE), 0).astype(f32)
        column = lax.broadcasted_iota(jnp.int32, (1, TILE), 1) % 64
        document = (column % 4).astype(f32)
        for blk in range(OWN):
            block = me + GROUP * blk
            here = lax.broadcasted_iota(jnp.int32, buckets.shape, 1) == block
            bucket = jnp.sum(jnp.where(here, buckets[...].astype(f32), 0.0), axis=1, keepdims=True)
            span = TILE * jnp.where(bucket == 0.0, 1.0, jnp.where(bucket == 1.0, 2.0, 4.0))
            slots = lengths[0].astype(f32)
            here = lax.broadcasted_iota(jnp.int32, slots.shape, 1) == block
            slots = jnp.sum(jnp.where(here, slots, 0.0), axis=1, keepdims=True)
            real = jnp.zeros((1, TILE), f32)
            for slot in range(4):
                real = jnp.where(document == slot, slots[slot : slot + 1], real)
            start = document * span
            inside = (row >= start) & (row < start + span)
            live = inside & (row < start + real)
            dead = inside & (row >= start + real)
            marks[blk, 0] = jnp.where(column < 4, live.astype(f32), jnp.where(column < 8, dead.astype(f32), 0.0)).astype(bf16)
            marks[blk, 1] = jnp.where(
                column < 4, jnp.where(inside, 0.0, MASKED), jnp.where(column < 8, MASKED, 0.0)
            ).astype(bf16)

        for copy in tab_moves:
            copy.wait()
        bucket_rows = [bucket_of(skew_offsets(tile)) for tile in (-1, 0, 1)]
        for group in range(GROUP):
            rows = tabs[group]
            for tile in range(3):
                values = jnp.zeros((8, 2 * TILE), f32)
                for bucket in range(BUCKETS):
                    values = jnp.where(bucket_rows[tile] == bucket, rows[:, bucket : bucket + 1], values)
                for at in range(3):
                    wide = jnp.broadcast_to(values[at : at + 1], (TILE, 2 * TILE))
                    wide = pltpu.roll(wide, 0, 1, stride=1, stride_axis=0)
                    tiles[3 * group + at, 1 + tile] = wide[:, :TILE]
            for at in range(3):
                tiles[3 * group + at, 0] = jnp.broadcast_to(rows[at : at + 1, 15:16], (TILE, TILE))
                tiles[3 * group + at, 4] = jnp.broadcast_to(rows[at : at + 1, 31:32], (TILE, TILE))

        for copy in weights:
            copy.wait()
        for blk in range(OWN):
            x_own[blk].wait()
            moves[blk][2].wait()
            project(blk, y)

        kept = []
        for blk in range(OWN):
            for at, (src, dst) in enumerate(((qs, q_kept), (ks, k_kept), (vs, v_kept))):
                kept.append(pltpu.make_async_copy(src.at[blk], dst.at[blk], keep_sem.at[blk, at]))

        def probs_copy(n):
            return pltpu.make_async_copy(ps.at[n % SLOTS], p_kept.at[n], p_sem.at[n % SLOTS])

        for blk in range(OWN):
            moves[blk][0].wait()
            moves[blk][1].wait()
            if blk == OWN - 1:
                for copies in cot_moves:
                    for copy in copies:
                        copy.start()
            project(blk, 1 - y)
            for copy in kept[3 * blk : 3 * blk + 3]:
                copy.start()

            def attend(pair, carry):
                n = blk * PAIRS + pair
                slot = n % SLOTS

                @pl.when(n >= SLOTS)
                def _():
                    probs_copy(n - SLOTS).wait()

                lanes = pl.ds(pl.multiple_of(pair * TILE, TILE), TILE)
                q, k, v = qs[blk, :, lanes], ks[blk, :, lanes], vs[blk, :, lanes]
                seen, sees = marks[blk, 0], marks[blk, 1]
                keys = (k * low + seen * high, k * high + seen * low)
                queries = (q * low + sees * high, q * high + sees * low)
                values = ((v * low + high).T, (v * high + low).T)
                scores = [None, None]
                parts = [None, None]

                def score(e):
                    scores[e] = nt(keys[e], queries[e])

                def soften(e):
                    head = 2 * pair + e
                    for qt in range(4):
                        at_q = slice(TILE * qt, TILE * qt + TILE)
                        block = []
                        for kt in range(4):
                            kind = min(max(kt - qt, -2), 2) + 2
                            block.append(scores[e][TILE * kt : TILE * kt + TILE, at_q] + tiles[head, kind])
                        peak = jnp.maximum(jnp.maximum(block[0], block[1]), jnp.maximum(block[2], block[3]))
                        peak = jnp.max(peak, axis=0, keepdims=True)
                        for kt in range(4):
                            ps[slot, e, TILE * kt : TILE * kt + TILE, at_q] = jnp.exp(block[kt] - peak).astype(bf16)

                def gather(e):
                    parts[e] = nn(values[e], ps[slot, e])

                score(0)
                score(1)
                soften(0)
                gather(0)
                soften(1)
                gather(1)
                scale = (1.0 / parts[0][64:65], 1.0 / parts[1][0:1])
                found = jnp.concatenate([parts[0][:64] * scale[0], parts[1][64:] * scale[1]], axis=0)
                cs[blk, :, lanes] = found.astype(bf16).T
                for e in range(2):
                    invs[blk, pair, e : e + 1] = scale[e]
                probs_copy(n).start()
                return carry

            lax.fori_loop(0, PAIRS, attend, 0)
        for n in range(OWN * PAIRS - SLOTS, OWN * PAIRS):
            probs_copy(n).wait()
        for copy in kept:
            copy.wait()

    pl.run_scoped(
        attention,
        qs=pltpu.VMEM((OWN, BLOCK, D), bf16),
        ks=pltpu.VMEM((OWN, BLOCK, D), bf16),
        vs=pltpu.VMEM((OWN, BLOCK, D), bf16),
        ps=pltpu.VMEM((SLOTS, 2, BLOCK, BLOCK), bf16),
        wq=pltpu.VMEM((D, D), bf16),
        wk=pltpu.VMEM((D, D), bf16),
        wv=pltpu.VMEM((D, D), bf16),
        tiles=pltpu.VMEM((HEADS, 5, TILE, TILE), f32),
        marks=pltpu.VMEM((OWN, 2, BLOCK, TILE), bf16),
        w_sem=DMA((3,)),
        keep_sem=DMA((OWN, 3)),
        p_sem=DMA((SLOTS,)),
    )

    def send_back(rows_of, result, at_blk, sems_at, which=(0, 1, 2, 3)):
        copies = []
        for at in which:
            owner = peers[at] if at < 3 else me
            source, target = rows_of.at[at_blk, mine(owner)], result.at[me + GROUP * at_blk]
            if at < 3:
                sems = (out_send.at[sems_at, at_blk, at], out_recv.at[sems_at, at_blk, at])
                copies.append(remote(source, target, *sems, {"head": owner}))
            else:
                copies.append(pltpu.make_async_copy(source, target, out_own.at[sems_at, at_blk]))
        return copies

    def start_back(rows_of, result, at_blk, sems_at):
        for copy in send_back(rows_of, result, at_blk, sems_at):
            copy.start()

    def wait_back(rows_of, result, sems_at):
        for blk in range(OWN):
            for copy in send_back(rows_of, result, blk, sems_at):
                copy.wait()

    def ffn_base(item, kind):
        return (item * 2 + kind) * 4

    def core_copies(item):
        if item < STEPS:
            copies = [
                remote(own.at[pl.ds(ffn_base(item, 1 - c), 4)], c_ffn.at[item], cs_send.at[item], cs_recv.at[item], partner["c"])
            ]
        else:
            g = item - STEPS
            copies = [
                remote(
                    own.at[ffn_base(g, 1 - c) + 2 * half + (1 - c)], c_att.at[g, half],
                    ca_send.at[g, half], ca_recv.at[g, half], partner["c"],
                )
                for half in range(2)
            ]
        return copies

    def add_into(target, arrived):
        target[...] = target[...] + arrived[...]

    def core_finish(item):
        for copy in core_copies(item):
            copy.wait()
        if item < STEPS:
            base = ffn_base(item, c)

            def add(at, carry):
                for b in range(2):
                    add_into(own.at[base + at, b], c_ffn.at[item, at, b])
                return carry

            lax.fori_loop(0, 4, add, 0)
        else:
            g = item - STEPS
            for half in range(2):
                slot = ffn_base(g, 1 - c) + 2 * half + c

                def add(b, carry):
                    add_into(own.at[slot, b], c_att.at[g, half, b])
                    return carry

                lax.fori_loop(0, 2, add, 0)

    def part(item, half, done, axis=None, value=None):
        index = []
        for name in ("z1", "z0", "x", "y"):
            if name == axis:
                index.append(value)
            elif name in done:
                index.append(place[name])
            else:
                index.append(slice(None))
        if item < STEPS:
            lead = pl.ds(ffn_base(item, c) + 2 * half, 2)
        else:
            lead = ffn_base(item - STEPS, 1 - c) + 2 * half + c
        return own.at[tuple([lead] + index)]

    stage_ffn = (r0_ffn, r1_ffn, r2_ffn, r3_ffn)
    stage_att = (r0_att, r1_att, r2_att, r3_att)

    def arrived_at(item, half, stage):
        if item < STEPS:
            return stage_ffn[stage].at[item, half]
        return stage_att[stage].at[item - STEPS, half]

    def stage_copies(item, stage):
        copies = []
        for half in range(2):
            order = ORDERS[item][half]
            axis = order[stage]
            copy = remote(
                part(item, half, order[:stage], axis, 1 - place[axis]), arrived_at(item, half, stage),
                st_send.at[item, half, stage], st_recv.at[item, half, stage], partner[axis],
            )
            copies.append(copy)
        return copies

    def stage_finish(item, stage):
        copies = stage_copies(item, stage)
        for half in range(2):
            copies[half].wait()
            order = ORDERS[item][half]
            kept = part(item, half, order[: stage + 1])
            arrived = arrived_at(item, half, stage)
            if stage < 3:
                add_into(kept, arrived)
            elif item < STEPS:
                f_ffn[item, half] = kept[...] + arrived[...]
            else:
                f_att[item - STEPS, half] = kept[...] + arrived[...]

    def fix_copies(item):
        if item < STEPS:
            copy = remote(f_ffn.at[item, 1 - c], rf_ffn.at[item], fx_send.at[item], fx_recv.at[item], partner["c"])
        else:
            g = item - STEPS
            copy = remote(f_att.at[g], rf_att.at[g], fx_send.at[item], fx_recv.at[item], partner["c"])
        return [copy]

    taken = []

    def advance(item, step):
        taken.append((item, step))
        if step == 2:
            core_finish(item)
        elif 3 <= step < 7:
            stage_finish(item, step - 3)
        if step == 1:
            copies = core_copies(item)
        elif step < 6:
            copies = stage_copies(item, step - 2)
        else:
            copies = fix_copies(item)
        for copy in copies:
            if step == 7:
                copy.wait()
            else:
                copy.start()

    def take(steps):
        for item, step in steps:
            if item == "out":
                send_back(cots, output, step // 3, 0, (step % 3,))[0].start()
            else:
                advance(item, step)

    def point(name):
        take(PLAN.get(name, ()))

    def within(name, at, first, last):
        for value in range(first, last):
            steps = PLAN.get(name + "." + str(value))
            if steps:

                @pl.when(at == value)
                def _():
                    take(steps)

    def project_out(at, carry):
        blk, half = at // 2, at % 2
        rows = pl.ds(pl.multiple_of(half * 256, 256), 256)
        hidden[blk, rows, :] = xs[blk, rows, :].astype(f32) + nn(cs[blk, rows, :], wo[...])
        return carry

    def feed_forward(nf, act, dinner, win, wback, w_sem):
        def fetch(step):
            slot = step % 2
            copies = []
            for f in range(8):
                at = f * (FF // 8) + step * TILE
                into = pl.ds(f * TILE, TILE)
                copies.append(pltpu.make_async_copy(w_in.at[:, pl.ds(at, TILE)], win.at[slot, :, into], w_sem.at[slot, 0, f]))
                copies.append(pltpu.make_async_copy(w_back.at[pl.ds(at, TILE)], wback.at[slot, into], w_sem.at[slot, 1, f]))
            for copy in copies:
                copy.start()
            return copies

        fetched = [fetch(0), fetch(1)]
        wo_copy.wait()
        lax.fori_loop(0, 4, project_out, 0)

        def norm(at, carry):
            blk, half = at // 2, at % 2
            rows = pl.ds(pl.multiple_of(half * 256, 256), 256)
            h = hidden[blk, rows, :]
            r = lax.rsqrt(jnp.mean(h * h, axis=-1, keepdims=True) + EPSILON)
            nf[blk, rows, :] = (h * r * gain_f[...].reshape(1, D)).astype(bf16)
            return carry

        lax.fori_loop(0, 4, norm, 0)
        for blk in range(OWN):
            c_own[blk].wait()
            for copy in cot_moves[blk]:
                copy.wait()

        for step in range(STEPS):
            slot = step % 2
            for copy in fetched[step]:
                copy.wait()

            def rows_of(at, carry):
                blk, half = at // 2, at % 2
                rows = pl.ds(pl.multiple_of(half * 256, 256), 256)
                within("rows" + str(step), at, 0, 4)
                v = nn(nf[blk, rows, :], win[slot])
                square = v * v
                t = jnp.tanh(GELU_A * v * (1.0 + GELU_B * square))
                a = (0.5 * v * (1.0 + t)).astype(bf16)
                slope = 0.5 * (1.0 + t) + 0.5 * GELU_A * v * (1.0 - t * t) * (1.0 + 3.0 * GELU_B * square)
                act[blk, rows, :] = a
                g = (nt(cots[blk, rows, :], wback[slot]) * slope).astype(bf16)
                dinner[blk, rows, :] = g
                onward = nn(a, wback[slot])
                backward = nt(g, win[slot])
                if step == 0:
                    total[blk, rows, :] = hidden[blk, rows, :] + onward
                    back[blk, rows, :] = backward
                else:
                    total[blk, rows, :] += onward
                    back[blk, rows, :] += backward
                return carry

            lax.fori_loop(0, 4, rows_of, 0)
            point("mid" + str(step) + ".0")
            if step + 2 < STEPS:
                fetched.append(fetch(step + 2))
            for b in range(2):
                if b == 1:
                    point("mid" + str(step) + ".b")
                res = tn(flat(nf), flat(dinner, slice(512 * b, 512 * b + 512))).astype(bf16)
                for m in range(4):
                    own[ffn_base(step, 0) + m, :, :, :, b] = res[:, TILE * m : TILE * m + TILE].reshape(2, 2, 2, 96, TILE)
            point("mid" + str(step) + ".1")
            for b in range(2):
                if b == 1:
                    point("mid" + str(step) + ".c")
                res = tn(flat(cots, slice(384 * b, 384 * b + 384)), flat(act)).astype(bf16)
                for m in range(4):
                    for f in range(8):
                        own[ffn_base(step, 1) + m, f // 4, (f // 2) % 2, f % 2, b] = res[
                            96 * m : 96 * m + 96, TILE * f : TILE * f + TILE
                        ]
            point("ffn" + str(step))

    pl.run_scoped(
        feed_forward,
        nf=pltpu.VMEM((OWN, BLOCK, D), bf16),
        act=pltpu.VMEM((OWN, BLOCK, 1024), bf16),
        dinner=pltpu.VMEM((OWN, BLOCK, 1024), bf16),
        win=pltpu.VMEM((2, D, 1024), bf16),
        wback=pltpu.VMEM((2, 1024, D), bf16),
        w_sem=DMA((2, 2, 8)),
    )

    small[0] = jnp.zeros((32, TILE), f32)
    buckets_acc[...] = jnp.zeros_like(buckets_acc)

    def attention_gradients(qs, ks, vs, ps, dsb, acc, far_acc, wq, wk, wv, l_sem, p_sem):
        more = []
        for at, (src, dst) in enumerate(((q_kept, qs), (k_kept, ks), (v_kept, vs), (w_q, wq), (w_k, wk), (w_v, wv))):
            copy = pltpu.make_async_copy(src, dst, l_sem.at[at])
            copy.start()
            more.append(copy)

        def pair_of(at):
            return at // 2 + 3 * (at % 2)

        def probs_copy(n):
            blk, at = n // PAIRS, n % PAIRS
            return pltpu.make_async_copy(p_kept.at[blk * PAIRS + pair_of(at)], ps.at[n % 2], p_sem.at[n % 2])

        probs_copy(0).start()

        which = lax.broadcasted_iota(jnp.int32, (2 * HEADS, D), 0) % HEADS
        spread = (lax.broadcasted_iota(jnp.int32, (2 * HEADS, D), 1) // 64 == which).astype(bf16)

        def close(at, gains):
            blk, half = at // 2, at % 2
            rows = pl.ds(pl.multiple_of(half * 256, 256), 256)
            within("close", at, 0, 4)
            h = hidden[blk, rows, :]
            r = lax.rsqrt(jnp.mean(h * h, axis=-1, keepdims=True) + EPSILON)
            d = back[blk, rows, :]
            scaled = gain_f[...].reshape(1, D) * d
            inner = jnp.mean(h * scaled, axis=-1, keepdims=True)
            grad = cots[blk, rows, :].astype(f32) + r * scaled - h * (r * r * r * inner)
            cots[blk, rows, :] = total[blk, rows, :].astype(bf16)
            hidden[blk, rows, :] = grad
            low_grad = grad.astype(bf16)
            scale = invs[blk, :, 0:2, rows].reshape(HEADS, 256).T
            coarse = scale.astype(bf16)
            scale = jnp.concatenate([coarse, (scale - coarse.astype(f32)).astype(bf16)], axis=1)
            passed = nt(low_grad, wo[...]).astype(bf16)
            dcs[blk, rows, :] = (passed.astype(f32) * nn(scale, spread)).astype(bf16)
            return gains + jnp.sum(d * h * r, axis=0, keepdims=True)

        gains = lax.fori_loop(0, 4, close, jnp.zeros((1, D), f32))
        for m in range(6):
            small[0, 22 + m : 23 + m, :] = gains[:, TILE * m : TILE * m + TILE]
        for blk in range(OWN):
            send_back(cots, output, blk, 0, (3,))[0].start()
        point("closed")
        for copy in more:
            copy.wait()

        lane = lax.broadcasted_iota(jnp.int32, (1, TILE), 1)
        is_low = lane < 64
        first_lane, second_lane = (lane % 64 == 0).astype(bf16), (lane % 64 == 1).astype(bf16)
        source = lax.broadcasted_iota(jnp.int32, (2 * TILE, TILE), 0) // 64 % 2
        swap = (source != lax.broadcasted_iota(jnp.int32, (2 * TILE, TILE), 1) // 64).astype(bf16)
        corner = lax.broadcasted_iota(jnp.int32, (TILE, TILE), 0) + lax.broadcasted_iota(jnp.int32, (TILE, TILE), 1)
        flip = (corner == TILE - 1).astype(bf16)

        def split(value):
            coarse = value.astype(bf16)
            return coarse, (value - coarse.astype(f32)).astype(bf16)

        def attention_back(blk, order, start):
            n = blk * PAIRS + order
            pair = pair_of(order)
            slot = n % 2
            probs_copy(n).wait()

            @pl.when(n + 1 < OWN * PAIRS)
            def _():
                probs_copy(n + 1).start()

            lanes = pl.ds(pl.multiple_of(pair * TILE, TILE), TILE)
            q, k, v, dc = qs[blk, :, lanes], ks[blk, :, lanes], vs[blk, :, lanes], dcs[blk, :, lanes]
            product = dc.astype(f32) * cs[blk, :, lanes].astype(f32)
            delta = nn(jnp.concatenate(split(product), axis=1), swap)
            coarse, fine = split(delta)
            delta = -(coarse * first_lane + fine * second_lane)
            left = (v * low + high, v * high + low)
            right = (dc * low + delta * high, dc * high + delta * low)
            grads = [nt(left[e], right[e]) for e in range(2)]
            found = [None, None]

            def scores_back(e):
                sums = {}
                for qt in range(4):
                    at_q = slice(TILE * qt, TILE * qt + TILE)
                    for kt in range(4):
                        at_k = slice(TILE * kt, TILE * kt + TILE)
                        ds = ps[slot, e, at_k, at_q].astype(f32) * grads[e][at_k, at_q]
                        dsb[e, at_k, at_q] = ds.astype(bf16)
                        sums.setdefault(min(max(kt - qt, -2), 2) + 2, []).append(ds)
                for kind, tiles in sums.items():
                    total_tile = tiles[0]
                    for tile in tiles[1:]:
                        total_tile = total_tile + tile
                    if kind in (0, 4):
                        total_tile = jnp.sum(total_tile.reshape(16, 8, TILE), axis=0)
                        at = (2 * pair + e, kind // 4)
                        far_acc[at] = total_tile if start else far_acc[at] + total_tile
                    else:
                        at = (2 * pair + e, kind - 1)
                        acc[at] = total_tile if start else acc[at] + total_tile

            def products(e):
                rows = slice(64 * e, 64 * e + 64)
                found[e] = (nn(k.T[rows], dsb[e]), nn(dsb[e], q), nn(ps[slot, e], dc))

            scores_back(0)
            products(0)
            scores_back(1)
            products(1)
            qs[blk, :, lanes] = jnp.concatenate([found[0][0], found[1][0]], axis=0).astype(bf16).T
            ks[blk, :, lanes] = jnp.where(is_low, found[0][1], found[1][1]).astype(bf16)
            vs[blk, :, lanes] = jnp.where(is_low, found[0][2], found[1][2]).astype(bf16)

        def first_norm(at, gains):
            blk, half = at // 2, at % 2
            rows = pl.ds(pl.multiple_of(half * 256, 256), 256)
            within("norm0", at, 0, 2)
            within("norm1", at - 2, 0, 2)
            d = nt(qs[blk, rows, :], wq[...]) + nt(ks[blk, rows, :], wk[...]) + nt(vs[blk, rows, :], wv[...])
            h = xs[blk, rows, :].astype(f32)
            r = lax.rsqrt(jnp.mean(h * h, axis=-1, keepdims=True) + EPSILON)
            scaled = gain_a[...].reshape(1, D) * d
            inner = jnp.mean(h * scaled, axis=-1, keepdims=True)
            xs[blk, rows, :] = (hidden[blk, rows, :] + r * scaled - h * (r * r * r * inner)).astype(bf16)
            return gains + jnp.sum(d * h * r, axis=0, keepdims=True)

        def first_block(order, carry):
            within("first", order, 0, PAIRS)
            attention_back(0, order, True)
            return carry

        lax.fori_loop(0, PAIRS, first_block, 0)
        gains = lax.fori_loop(0, 2, first_norm, jnp.zeros((1, D), f32))
        start_back(xs, grad_tokens, 0, 1)
        point("GT0")

        for group in range(3):
            def second_block(order, carry):
                within("second" + str(group), order - 2 * group, 0, 2)
                attention_back(1, order, False)
                return carry

            lax.fori_loop(2 * group, 2 * group + 2, second_block, 0)
            point("second" + str(group) + ".2")
            for side in range(2):
                if side == 1:
                    point("side" + str(group))
                pair = group + 3 * side
                lanes = slice(TILE * pair, TILE * pair + TILE)
                qk = tn(flat(ns), jnp.concatenate([flat(t, lanes) for t in (qs, ks)], axis=1)).astype(bf16)
                grad_v = tn(flat(ns), flat(vs, lanes)).astype(bf16)
                grad_o = tn(flat(cs), flat(hidden, lanes).astype(bf16)).astype(bf16)
                pieces = ((qk[:, :TILE], qk[:, TILE:]), (grad_v, grad_o))
                base = ffn_base(group, 1 - c)
                for kind in range(2):
                    for half in range(2):
                        own[base + 2 * half + kind, :, :, :, side] = pieces[kind][half].reshape(2, 2, 2, 96, TILE)
            point("group" + str(group))

        def diagonals(head, carry):
            sums = []
            for tile in range(3):
                turned = nn(flip, jnp.concatenate(split(acc[head, tile]), axis=1))
                turned = turned[:, :TILE] + turned[:, TILE:]
                wide = jnp.concatenate([turned, jnp.zeros((TILE, TILE), f32)], axis=1)
                wide = pltpu.roll(wide, 0, 1, stride=1, stride_axis=0)
                sums.append(jnp.sum(wide, axis=0, keepdims=True))
            for kind in range(2):
                sums.append(jnp.sum(far_acc[head, kind], axis=0, keepdims=True))
            buckets_acc[pl.ds(head, 1), :] = jnp.concatenate(sums, axis=1)
            return carry

        gains = lax.fori_loop(2, 4, first_norm, gains)
        start_back(xs, grad_tokens, 1, 1)
        point("normed")
        lax.fori_loop(0, HEADS, diagonals, 0)
        for m in range(6):
            small[0, 16 + m : 17 + m, :] = gains[:, TILE * m : TILE * m + TILE]

    pl.run_scoped(
        attention_gradients,
        qs=pltpu.VMEM((OWN, BLOCK, D), bf16),
        ks=pltpu.VMEM((OWN, BLOCK, D), bf16),
        vs=pltpu.VMEM((OWN, BLOCK, D), bf16),
        ps=pltpu.VMEM((2, 2, BLOCK, BLOCK), bf16),
        dsb=pltpu.VMEM((2, BLOCK, BLOCK), bf16),
        acc=pltpu.VMEM((HEADS, 3, TILE, TILE), f32),
        far_acc=pltpu.VMEM((HEADS, 2, 8, TILE), f32),
        wq=pltpu.VMEM((D, D), bf16),
        wk=pltpu.VMEM((D, D), bf16),
        wv=pltpu.VMEM((D, D), bf16),
        l_sem=DMA((6,)),
        p_sem=DMA((2,)),
    )

    lane = lax.broadcasted_iota(jnp.int32, (1, 2 * TILE), 1)
    offsets = jnp.concatenate([TILE * tile + TILE - 1 - lane for tile in (-1, 0, 1)], axis=1)
    far = lax.broadcasted_iota(jnp.int32, (1, 256), 1)
    column = jnp.concatenate([bucket_of(offsets), jnp.where(far < TILE, 15, 31)], axis=1)
    hot = (lax.broadcasted_iota(jnp.int32, (TILE, 1024), 0) == column).astype(f32)
    small[0, 0:16, :] = lax.dot_general(
        buckets_acc[...], hot, (((1,), (1,)), ((), ())), preferred_element_type=f32, precision=lax.Precision.HIGHEST
    )
    copies = [
        remote(small.at[0], small_in.at[at], sm_send.at[at], sm_recv.at[at], {"head": peers[at]}) for at in range(3)
    ]
    for copy in copies:
        copy.start()
    point("small0")
    for copy in copies:
        copy.wait()
    small[1] = (small[0] + small_in[0]) + (small_in[1] + small_in[2])
    copies = [
        remote(small.at[1], small_far.at[at], sm_send.at[3 + at], sm_recv.at[3 + at], column_peers[at]) for at in range(7)
    ]
    for copy in copies:
        copy.start()
    point("small1")
    for copy in copies:
        copy.wait()
    total_small = small[1]
    for at in range(7):
        total_small = total_small + small_far[at]
    g_small[...] = total_small
    point("last")
    assert sorted(set(taken)) == [(item, step) for item in range(6) for step in range(1, 8)]
    wait_back(cots, output, 0)
    wait_back(xs, grad_tokens, 1)
    emit(c, f_ffn, rf_ffn, f_att, rf_att, (g_q, g_k, g_v, g_o), g_in, g_back)


def emit(c, f_ffn, rf_ffn, f_att, rf_att, g_square, g_in, g_back):
    first = c == 0
    for step in range(STEPS):
        for b in range(2):
            kept, got = f_ffn[step, c, b].astype(f32), rf_ffn[step, b].astype(f32)
            g_in[:, 384 * b + TILE * step : 384 * b + TILE * step + TILE] = jnp.where(first, kept, got)
            g_back[96 * b : 96 * b + 96, TILE * step : TILE * step + TILE] = jnp.where(first, got, kept)
    for half in range(2):
        for kind in range(2):
            pieces = []
            for g in range(3):
                kept, got = f_att[g, half].astype(f32), rf_att[g, half].astype(f32)
                pieces.append(jnp.where(first, kept, got) if kind == 0 else jnp.where(first, got, kept))
            wide = jnp.concatenate(pieces, axis=1)
            g_square[2 * kind + half][...] = jnp.where(first, wide[:, :192], wide[:, 192:])


def layer_call(outer, tokens, cot, table, buckets, lengths, w_q, w_k, w_v, w_o, w_in, w_back, gain_a, gain_f):
    rows = (OWN, BLOCK, D)
    local = jax.ShapeDtypeStruct((ROWS, TILE, D), bf16)
    square = jax.ShapeDtypeStruct((96, 192), f32)
    kept = jax.ShapeDtypeStruct(rows, bf16)
    halves = (3, 2)
    scratch = [
        pltpu.VMEM(rows, bf16),
        pltpu.VMEM(rows, bf16),
        pltpu.VMEM(rows, bf16),
        pltpu.VMEM(rows, bf16),
        pltpu.VMEM(rows, f32),
        pltpu.VMEM(rows, f32),
        pltpu.VMEM(rows, f32),
        pltpu.VMEM(rows, bf16),
        pltpu.VMEM((D, D), bf16),
        pltpu.VMEM((OWN, PAIRS, 8, BLOCK), f32),
        pltpu.VMEM((8, TILE), f32),
        pltpu.VMEM((GROUP, 8, TILE), f32),
        pltpu.VMEM((24,) + UNIT, bf16),
        pltpu.VMEM((3, 4) + UNIT, bf16),
        pltpu.VMEM((3, 2) + UNIT, bf16),
    ]
    for dims in ((2,), ()):
        for stage in range(4):
            scratch.append(pltpu.VMEM(halves + dims + (2,) * (3 - stage) + UNIT[4:], bf16))
    scratch += [
        pltpu.VMEM((3, 2, 2) + UNIT[4:], bf16),
        pltpu.VMEM((3, 2) + UNIT[4:], bf16),
        pltpu.VMEM((3, 2) + UNIT[4:], bf16),
        pltpu.VMEM((3, 2) + UNIT[4:], bf16),
        pltpu.VMEM((2, 32, TILE), f32),
        pltpu.VMEM((3, 32, TILE), f32),
        pltpu.VMEM((7, 32, TILE), f32),
        pltpu.VMEM((16, 1024), f32),
        DMA((OWN,)), DMA((OWN, 3)), DMA((OWN, 3)),
        DMA((OWN,)), DMA((OWN, 3)), DMA((OWN, 3)),
        DMA((3,)), DMA((3,)), DMA(()),
        DMA((3,)), DMA((3,)), DMA((3, 2)), DMA((3, 2)),
        DMA((6, 2, 4)), DMA((6, 2, 4)), DMA((6,)), DMA((6,)), DMA((10,)), DMA((10,)),
        DMA((2, OWN)), DMA((2, OWN, 3)), DMA((2, OWN, 3)),
    ]
    results = pl.pallas_call(
        functools.partial(layer_kernel, outer),
        out_shape=(
            local,
            local,
            square,
            square,
            square,
            square,
            jax.ShapeDtypeStruct((96, D), f32),
            jax.ShapeDtypeStruct((192, 384), f32),
            jax.ShapeDtypeStruct((32, TILE), f32),
            kept,
            kept,
            kept,
            jax.ShapeDtypeStruct((OWN * PAIRS, 2, BLOCK, BLOCK), bf16),
        ),
        in_specs=[ANY, ANY, VMEM, VMEM, VMEM] + [ANY] * 6 + [VMEM, VMEM],
        out_specs=(ANY, ANY) + (VMEM,) * 7 + (ANY,) * 4,
        scratch_shapes=scratch,
        compiler_params=pltpu.CompilerParams(collective_id=0, has_side_effects=True, vmem_limit_bytes=63 * 2**20),
    )(tokens, cot, table, buckets, lengths, w_q, w_k, w_v, w_o, w_in, w_back, gain_a, gain_f)
    return results[:9]


def settle_kernel(per, *refs):
    sources, small_in, outs, refs = refs[:8], refs[8], refs[9:20], refs[20:]
    held, (small, read, written, small_sem) = refs[:8], refs[8:]
    pieces = [(0, pl.ds(0, 4)), (0, pl.ds(4, 4)), (1, pl.ds(0, 4)), (1, pl.ds(4, 4))]
    pieces += [(at, slice(None)) for at in range(2, 8)]
    reads = [
        pltpu.make_async_copy(sources[at].at[rows], held[at].at[rows], read.at[n]) for n, (at, rows) in enumerate(pieces)
    ]
    writes = [
        pltpu.make_async_copy(held[at].at[rows], outs[at].at[rows], written.at[n]) for n, (at, rows) in enumerate(pieces)
    ]
    small_copy = pltpu.make_async_copy(small_in, small, small_sem)
    small_copy.start()
    for copy in reads:
        copy.start()
    small_copy.wait()
    me = lax.axis_index("head")

    def mine(options):
        value = options[0]
        for at in range(1, GROUP):
            value = jnp.where(me == at, options[at], value)
        return value

    share = D // GROUP
    for at in range(2):
        whole = jnp.concatenate([small[16 + 6 * at + m : 17 + 6 * at + m, :] for m in range(6)], axis=1)
        outs[8 + at][...] = mine([whole[:, share * j : share * j + share] for j in range(GROUP)]).reshape(share)
    rows = mine([small[per * j : per * j + per, :] for j in range(GROUP)])
    outs[10][...] = rows[:, 0:BUCKETS]
    for get, put in zip(reads, writes):
        get.wait()
        put.start()
    for put in writes:
        put.wait()


def settle_call(per, *values):
    large = values[:8]
    return pl.pallas_call(
        functools.partial(settle_kernel, per),
        out_shape=tuple(jax.ShapeDtypeStruct(v.shape, v.dtype) for v in large)
        + (jax.ShapeDtypeStruct((D // GROUP,), f32),) * 2
        + (jax.ShapeDtypeStruct((per, BUCKETS), f32),),
        in_specs=[ANY] * 9,
        out_specs=(ANY,) * 8 + (VMEM,) * 3,
        scratch_shapes=[pltpu.VMEM(v.shape, v.dtype) for v in values] + [DMA((10,)), DMA((10,)), DMA(())],
        compiler_params=pltpu.CompilerParams(vmem_limit_bytes=63 * 2**20),
    )(*values)


def shards(
    tokens, bucket_of_block, lengths, w_query, w_key, w_value, w_out, w_in, w_back, gain_attn, gain_ffn, bias_table, cotangent
):
    outer = lax.axis_size("dp") // 8
    per = bias_table.shape[1]
    slots = lengths.transpose(0, 2, 1)
    output, grad_tokens, *weights, small = layer_call(
        outer, tokens, cotangent, bias_table.T, bucket_of_block, slots,
        w_query, w_key, w_value, w_out, w_in, w_back, gain_attn, gain_ffn,
    )
    if outer > 1:
        groups = [[at * outer + spare for spare in range(outer)] for at in range(8)]
        weights = [
            lax.psum_scatter(grad, "dp", scatter_dimension=dim, axis_index_groups=groups, tiled=True)
            for grad, dim in zip(weights, (0, 0, 0, 0, 0, 1))
        ]
        small = lax.psum(small, "dp", axis_index_groups=groups)
    results = settle_call(per, output, grad_tokens, *weights, small)
    return results[:7] + (results[7].T,) + results[8:10] + (results[10].T,)


def solution(mesh):
    whole = P()
    rows = P("dp", "head", None)
    block = P("dp", "head")
    return jax.shard_map(
        shards,
        mesh=mesh,
        in_specs=(rows, P("dp", None), P("dp", None, None)) + (whole,) * 8 + (P(None, "head"), rows),
        out_specs=(rows, rows) + (block,) * 6 + (P("head"), P("head"), P(None, "head")),
        check_vma=False,
    )
```

```python
import functools
import math

import jax
import jax.numpy as jnp
from jax import lax
from jax.experimental import pallas as pl
from jax.experimental.pallas import tpu as pltpu
from jax.sharding import PartitionSpec as P

D = 768
HEADS = 12
FF = 3072
BUCKETS = 32
BLOCK = 512
PAIRS = 6
OWN = 2
GROUP = 4
ROWS = 8
EPSILON = 1e-06
TILE = 128
MASKED = -float(2**30)
GELU_A = math.sqrt(2.0 / math.pi)
GELU_B = 0.044715

bf16 = jnp.bfloat16
f32 = jnp.float32
MESH = pl.DeviceIdType.MESH
ANY = pl.BlockSpec(memory_space=pl.ANY)
VMEM = pl.BlockSpec(memory_space=pltpu.VMEM)
DMA = pltpu.SemaphoreType.DMA
STEPS = 3


def nn(left, right):
    return jnp.dot(left, right, preferred_element_type=f32)


def nt(left, right):
    return lax.dot_general(left, right, (((1,), (1,)), ((), ())), preferred_element_type=f32)


def tn(left, right):
    return lax.dot_general(left, right, (((0,), (0,)), ((), ())), preferred_element_type=f32)


def flat(ref, lanes=slice(None)):
    value = ref[:, :, lanes]
    return value.reshape(value.shape[0] * value.shape[1], value.shape[2])


def head_masks():
    lane = lax.broadcasted_iota(jnp.int32, (1, TILE), 1)
    low = (lane < TILE // 2).astype(f32)
    return low.astype(bf16), (1.0 - low).astype(bf16)


def bucket_of(offset):
    magnitude = jnp.abs(offset)
    far = jnp.full(offset.shape, 8, jnp.int32)
    for threshold in (12, 16, 23, 32, 46, 64, 91):
        far = far + (magnitude >= threshold).astype(jnp.int32)
    side = jnp.where(offset > 0, 16, 0).astype(jnp.int32)
    return side + jnp.where(magnitude < 8, magnitude, far)


def skew_offsets(tile):
    lane = lax.broadcasted_iota(jnp.int32, (1, 2 * TILE), 1)
    return TILE * tile + jnp.where(lane < TILE, -lane, 2 * TILE - lane)


ORDERS = (
    (("x", "z0", "z1", "y"), ("z0", "x", "y", "z1")),
    (("x", "z0", "z1", "y"), ("z0", "x", "y", "z1")),
    (("x", "z0", "z1", "y"), ("z0", "x", "y", "z1")),
    (("x", "z0", "z1", "y"), ("z0", "x", "y", "z1")),
    (("x", "z0", "z1", "y"), ("z0", "x", "y", "z1")),
    (("x", "z0", "z1", "y"), ("z0", "x", "y", "z1")),
)
UNIT = (2, 2, 2, 2, 96, TILE)
SLOTS = 4

PLAN = {
    "ffn0": [(0, 1)],
    "rows1.3": [(0, 2)],
    "ffn1": [(1, 1)],
    "rows2.3": [(0, 3), (1, 2)],
    "ffn2": [(2, 1)],
    "close.1": [(0, 4)],
    "closed": [("out", 0)],
    "first.1": [("out", 1), (2, 2)],
    "first.2": [("out", 2)],
    "first.3": [("out", 3)],
    "first.4": [("out", 4), (1, 3)],
    "first.5": [("out", 5)],
    "norm0.0": [(0, 5)],
    "side0": [(2, 3)],
    "group0": [(3, 1)],
    "second1.1": [(1, 4)],
    "side1": [(0, 6), (3, 2)],
    "group1": [(4, 1)],
    "second2.1": [(0, 7), (2, 4)],
    "second2.2": [(4, 2)],
    "group2": [(1, 5), (3, 3), (5, 1)],
    "small0": [(2, 5), (4, 3), (5, 2)],
    "small1": [(1, 6), (3, 4)],
    "last": [(1, 7), (4, 4), (2, 6), (5, 3), (2, 7), (3, 5), (4, 5), (5, 4), (3, 6), (4, 6), (3, 7), (5, 5), (4, 7), (5, 6), (5, 7)],
}


def layer_kernel(
    outer,
    tokens, cot, table, buckets, lengths, w_q, w_k, w_v, w_o, w_in, w_back, gain_a, gain_f,
    output, grad_tokens, g_q, g_k, g_v, g_o, g_in, g_back, g_small, q_kept, k_kept, v_kept, p_kept,
    xs, cots, ns, cs, hidden, total, back, dcs, wo, invs, tab, tabs, own,
    c_ffn, c_att, r0_ffn, r1_ffn, r2_ffn, r3_ffn, r0_att, r1_att, r2_att, r3_att,
    f_ffn, f_att, rf_ffn, rf_att, small, small_in, small_far, buckets_acc,
    own_sem, send_sem, recv_sem, cot_own, cot_send, cot_recv, tab_send, tab_recv, wo_sem,
    cs_send, cs_recv, ca_send, ca_recv, st_send, st_recv, fx_send, fx_recv, sm_send, sm_recv,
    out_own, out_send, out_recv,
):
    me = lax.axis_index("head")
    dp = lax.axis_index("dp")
    y, c = me // 2, me % 2
    chunk, spare = dp // outer, dp % outer
    z1, z0, x = chunk // 4, (chunk // 2) % 2, chunk % 2
    place = {"x": x, "y": y, "z0": z0, "z1": z1}

    def device(row, column):
        return {"dp": row * outer + spare, "head": column}

    partner = {
        "c": device(chunk, 2 * y + (1 - c)),
        "y": device(chunk, 2 * (1 - y) + c),
        "x": device(chunk + 1 - 2 * x, me),
        "z0": device(chunk + 2 - 4 * z0, me),
        "z1": device(chunk + 4 - 8 * z1, me),
    }
    peers = ((1 - y) * 2 + c, (1 - y) * 2 + (1 - c), y * 2 + (1 - c))
    column_peers = [device((chunk + at) % 8, me) for at in range(1, 8)]
    greeted = [{"head": peer} for peer in peers] + column_peers
    barrier = pltpu.get_barrier_semaphore()
    for other in greeted:
        pl.semaphore_signal(barrier, inc=1, device_id=other, device_id_type=MESH)

    def remote(src, dst, sends, recvs, other):
        return pltpu.make_async_remote_copy(
            src_ref=src, dst_ref=dst, send_sem=sends, recv_sem=recvs, device_id=other, device_id_type=MESH
        )

    def mine(start):
        return pl.ds(pl.multiple_of(start * TILE, TILE), TILE)

    x_own = [pltpu.make_async_copy(tokens.at[me + GROUP * blk], xs.at[blk, mine(me)], own_sem.at[blk]) for blk in range(OWN)]
    c_own = [pltpu.make_async_copy(cot.at[me + GROUP * blk], cots.at[blk, mine(me)], cot_own.at[blk]) for blk in range(OWN)]
    wo_copy = pltpu.make_async_copy(w_o, wo, wo_sem)
    for copy in x_own:
        copy.start()
    tab[...] = jnp.zeros_like(tab)
    tab[0 : table.shape[0], 0:BUCKETS] = table[...]
    tabs[me] = tab[...]
    pl.semaphore_wait(barrier, len(greeted))

    def send(source, dest, sends, recvs, blk, at):
        return remote(
            source.at[peers[at] + GROUP * blk], dest.at[blk, mine(me)], sends.at[blk, at], recvs.at[blk, at], {"head": peers[at]}
        )

    moves = [[send(tokens, xs, send_sem, recv_sem, blk, at) for at in range(3)] for blk in range(OWN)]
    cot_moves = [[send(cot, cots, cot_send, cot_recv, blk, at) for at in range(3)] for blk in range(OWN)]
    tab_moves = [remote(tab, tabs.at[me], tab_send.at[at], tab_recv.at[at], {"head": peers[at]}) for at in range(3)]
    for copy in tab_moves:
        copy.start()
    for copy in moves[0]:
        copy.start()

    low, high = head_masks()

    def attention(qs, ks, vs, ps, wq, wk, wv, tiles, marks, w_sem, keep_sem, p_sem):
        weights = [
            pltpu.make_async_copy(src, dst, w_sem.at[at])
            for at, (src, dst) in enumerate(((w_q, wq), (w_k, wk), (w_v, wv)))
        ]
        for copy in weights:
            copy.start()
        for copy in c_own:
            copy.start()
        wo_copy.start()

        def project(blk, half):
            rows = pl.ds(pl.multiple_of(half * 256, 256), 256)
            x = xs[blk, rows, :].astype(f32)
            r = lax.rsqrt(jnp.mean(x * x, axis=-1, keepdims=True) + EPSILON)
            normed = (x * r * gain_a[...].reshape(1, D)).astype(bf16)
            ns[blk, rows, :] = normed
            qs[blk, rows, :] = nn(normed, wq[...]).astype(bf16)
            ks[blk, rows, :] = nn(normed, wk[...]).astype(bf16)
            vs[blk, rows, :] = nn(normed, wv[...]).astype(bf16)

        row = lax.broadcasted_iota(jnp.int32, (BLOCK, TILE), 0).astype(f32)
        column = lax.broadcasted_iota(jnp.int32, (1, TILE), 1) % 64
        document = (column % 4).astype(f32)
        for blk in range(OWN):
            block = me + GROUP * blk
            here = lax.broadcasted_iota(jnp.int32, buckets.shape, 1) == block
            bucket = jnp.sum(jnp.where(here, buckets[...].astype(f32), 0.0), axis=1, keepdims=True)
            span = TILE * jnp.where(bucket == 0.0, 1.0, jnp.where(bucket == 1.0, 2.0, 4.0))
            slots = lengths[0].astype(f32)
            here = lax.broadcasted_iota(jnp.int32, slots.shape, 1) == block
            slots = jnp.sum(jnp.where(here, slots, 0.0), axis=1, keepdims=True)
            real = jnp.zeros((1, TILE), f32)
            for slot in range(4):
                real = jnp.where(document == slot, slots[slot : slot + 1], real)
            start = document * span
            inside = (row >= start) & (row < start + span)
            live = inside & (row < start + real)
            dead = inside & (row >= start + real)
            marks[blk, 0] = jnp.where(column < 4, live.astype(f32), jnp.where(column < 8, dead.astype(f32), 0.0)).astype(bf16)
            marks[blk, 1] = jnp.where(
                column < 4, jnp.where(inside, 0.0, MASKED), jnp.where(column < 8, MASKED, 0.0)
            ).astype(bf16)

        for copy in tab_moves:
            copy.wait()
        bucket_rows = [bucket_of(skew_offsets(tile)) for tile in (-1, 0, 1)]
        for group in range(GROUP):
            rows = tabs[group]
            for tile in range(3):
                values = jnp.zeros((8, 2 * TILE), f32)
                for bucket in range(BUCKETS):
                    values = jnp.where(bucket_rows[tile] == bucket, rows[:, bucket : bucket + 1], values)
                for at in range(3):
                    wide = jnp.broadcast_to(values[at : at + 1], (TILE, 2 * TILE))
                    wide = pltpu.roll(wide, 0, 1, stride=1, stride_axis=0)
                    tiles[3 * group + at, 1 + tile] = wide[:, :TILE]
            for at in range(3):
                tiles[3 * group + at, 0] = jnp.broadcast_to(rows[at : at + 1, 15:16], (TILE, TILE))
                tiles[3 * group + at, 4] = jnp.broadcast_to(rows[at : at + 1, 31:32], (TILE, TILE))

        for copy in weights:
            copy.wait()
        for blk in range(OWN):
            x_own[blk].wait()
        moves[0][2].wait()
        project(0, y)
        for copy in moves[0][:2]:
            copy.wait_send()
        for copy in moves[1]:
            copy.start()
        moves[1][2].wait_recv()
        project(1, y)

        kept = []
        for blk in range(OWN):
            for at, (src, dst) in enumerate(((qs, q_kept), (ks, k_kept), (vs, v_kept))):
                kept.append(pltpu.make_async_copy(src.at[blk], dst.at[blk], keep_sem.at[blk, at]))

        def probs_copy(n):
            return pltpu.make_async_copy(ps.at[n % SLOTS], p_kept.at[n], p_sem.at[n % SLOTS])

        for blk in range(OWN):
            for at in range(2):
                moves[blk][at].wait_recv()
            project(blk, 1 - y)
            for copy in kept[3 * blk : 3 * blk + 3]:
                copy.start()

            def attend(pair, carry):
                n = blk * PAIRS + pair

                @pl.when(pair == 3)
                def _():
                    for copy in (moves[1], cot_moves[0])[blk]:
                        copy.wait_send()
                    for copy in cot_moves[blk]:
                        copy.start()

                slot = n % SLOTS

                @pl.when(n >= SLOTS)
                def _():
                    probs_copy(n - SLOTS).wait()

                lanes = pl.ds(pl.multiple_of(pair * TILE, TILE), TILE)
                q, k, v = qs[blk, :, lanes], ks[blk, :, lanes], vs[blk, :, lanes]
                seen, sees = marks[blk, 0], marks[blk, 1]
                keys = (k * low + seen * high, k * high + seen * low)
                queries = (q * low + sees * high, q * high + sees * low)
                values = ((v * low + high).T, (v * high + low).T)
                scores = [None, None]
                parts = [None, None]

                def score(e):
                    scores[e] = nt(keys[e], queries[e])

                def soften(e):
                    head = 2 * pair + e
                    for qt in range(4):
                        at_q = slice(TILE * qt, TILE * qt + TILE)
                        block = []
                        for kt in range(4):
                            kind = min(max(kt - qt, -2), 2) + 2
                            block.append(scores[e][TILE * kt : TILE * kt + TILE, at_q] + tiles[head, kind])
                        peak = jnp.maximum(jnp.maximum(block[0], block[1]), jnp.maximum(block[2], block[3]))
                        peak = jnp.max(peak, axis=0, keepdims=True)
                        for kt in range(4):
                            ps[slot, e, TILE * kt : TILE * kt + TILE, at_q] = jnp.exp(block[kt] - peak).astype(bf16)

                def gather(e):
                    parts[e] = nn(values[e], ps[slot, e])

                score(0)
                score(1)
                soften(0)
                gather(0)
                soften(1)
                gather(1)
                scale = (1.0 / parts[0][64:65], 1.0 / parts[1][0:1])
                found = jnp.concatenate([parts[0][:64] * scale[0], parts[1][64:] * scale[1]], axis=0)
                cs[blk, :, lanes] = found.astype(bf16).T
                for e in range(2):
                    invs[blk, pair, e : e + 1] = scale[e]
                probs_copy(n).start()
                return carry

            lax.fori_loop(0, PAIRS, attend, 0)
        for n in range(OWN * PAIRS - SLOTS, OWN * PAIRS):
            probs_copy(n).wait()
        for copy in kept:
            copy.wait()

    pl.run_scoped(
        attention,
        qs=pltpu.VMEM((OWN, BLOCK, D), bf16),
        ks=pltpu.VMEM((OWN, BLOCK, D), bf16),
        vs=pltpu.VMEM((OWN, BLOCK, D), bf16),
        ps=pltpu.VMEM((SLOTS, 2, BLOCK, BLOCK), bf16),
        wq=pltpu.VMEM((D, D), bf16),
        wk=pltpu.VMEM((D, D), bf16),
        wv=pltpu.VMEM((D, D), bf16),
        tiles=pltpu.VMEM((HEADS, 5, TILE, TILE), f32),
        marks=pltpu.VMEM((OWN, 2, BLOCK, TILE), bf16),
        w_sem=DMA((3,)),
        keep_sem=DMA((OWN, 3)),
        p_sem=DMA((SLOTS,)),
    )

    def send_back(rows_of, result, at_blk, sems_at, which=(0, 1, 2, 3)):
        copies = []
        for at in which:
            owner = peers[at] if at < 3 else me
            source, target = rows_of.at[at_blk, mine(owner)], result.at[me + GROUP * at_blk]
            if at < 3:
                sems = (out_send.at[sems_at, at_blk, at], out_recv.at[sems_at, at_blk, at])
                copies.append(remote(source, target, *sems, {"head": owner}))
            else:
                copies.append(pltpu.make_async_copy(source, target, out_own.at[sems_at, at_blk]))
        return copies

    def start_back(rows_of, result, at_blk, sems_at):
        for copy in send_back(rows_of, result, at_blk, sems_at):
            copy.start()

    def wait_back(rows_of, result, sems_at):
        for blk in range(OWN):
            for copy in send_back(rows_of, result, blk, sems_at):
                copy.wait()

    def ffn_base(item, kind):
        return (item * 2 + kind) * 4

    def core_copies(item):
        if item < STEPS:
            copies = [
                remote(own.at[pl.ds(ffn_base(item, 1 - c), 4)], c_ffn.at[item], cs_send.at[item], cs_recv.at[item], partner["c"])
            ]
        else:
            g = item - STEPS
            copies = [
                remote(
                    own.at[ffn_base(g, 1 - c) + 2 * half + (1 - c)], c_att.at[g, half],
                    ca_send.at[g, half], ca_recv.at[g, half], partner["c"],
                )
                for half in range(2)
            ]
        return copies

    def add_into(target, arrived):
        target[...] = target[...] + arrived[...]

    def core_finish(item):
        for copy in core_copies(item):
            copy.wait()
        if item < STEPS:
            base = ffn_base(item, c)

            def add(at, carry):
                for b in range(2):
                    add_into(own.at[base + at, b], c_ffn.at[item, at, b])
                return carry

            lax.fori_loop(0, 4, add, 0)
        else:
            g = item - STEPS
            for half in range(2):
                slot = ffn_base(g, 1 - c) + 2 * half + c

                def add(b, carry):
                    add_into(own.at[slot, b], c_att.at[g, half, b])
                    return carry

                lax.fori_loop(0, 2, add, 0)

    def part(item, half, done, axis=None, value=None):
        index = []
        for name in ("z1", "z0", "x", "y"):
            if name == axis:
                index.append(value)
            elif name in done:
                index.append(place[name])
            else:
                index.append(slice(None))
        if item < STEPS:
            lead = pl.ds(ffn_base(item, c) + 2 * half, 2)
        else:
            lead = ffn_base(item - STEPS, 1 - c) + 2 * half + c
        return own.at[tuple([lead] + index)]

    stage_ffn = (r0_ffn, r1_ffn, r2_ffn, r3_ffn)
    stage_att = (r0_att, r1_att, r2_att, r3_att)

    def arrived_at(item, half, stage):
        if item < STEPS:
            return stage_ffn[stage].at[item, half]
        return stage_att[stage].at[item - STEPS, half]

    def stage_copies(item, stage):
        copies = []
        for half in range(2):
            order = ORDERS[item][half]
            axis = order[stage]
            copy = remote(
                part(item, half, order[:stage], axis, 1 - place[axis]), arrived_at(item, half, stage),
                st_send.at[item, half, stage], st_recv.at[item, half, stage], partner[axis],
            )
            copies.append(copy)
        return copies

    def stage_finish(item, stage):
        copies = stage_copies(item, stage)
        for half in range(2):
            copies[half].wait()
            order = ORDERS[item][half]
            kept = part(item, half, order[: stage + 1])
            arrived = arrived_at(item, half, stage)
            if stage < 3:
                add_into(kept, arrived)
            elif item < STEPS:
                f_ffn[item, half] = kept[...] + arrived[...]
            else:
                f_att[item - STEPS, half] = kept[...] + arrived[...]

    def fix_copies(item):
        if item < STEPS:
            copy = remote(f_ffn.at[item, 1 - c], rf_ffn.at[item], fx_send.at[item], fx_recv.at[item], partner["c"])
        else:
            g = item - STEPS
            copy = remote(f_att.at[g], rf_att.at[g], fx_send.at[item], fx_recv.at[item], partner["c"])
        return [copy]

    taken = []

    def advance(item, step):
        taken.append((item, step))
        if step == 2:
            core_finish(item)
        elif 3 <= step < 7:
            stage_finish(item, step - 3)
        if step == 1:
            copies = core_copies(item)
        elif step < 6:
            copies = stage_copies(item, step - 2)
        else:
            copies = fix_copies(item)
        for copy in copies:
            if step == 7:
                copy.wait()
            else:
                copy.start()

    def take(steps):
        for item, step in steps:
            if item == "out":
                send_back(cots, output, step // 3, 0, (step % 3,))[0].start()
            else:
                advance(item, step)

    def point(name):
        take(PLAN.get(name, ()))

    def within(name, at, first, last):
        for value in range(first, last):
            steps = PLAN.get(name + "." + str(value))
            if steps:

                @pl.when(at == value)
                def _():
                    take(steps)

    def project_out(at, carry):
        blk, half = at // 2, at % 2
        rows = pl.ds(pl.multiple_of(half * 256, 256), 256)
        hidden[blk, rows, :] = xs[blk, rows, :].astype(f32) + nn(cs[blk, rows, :], wo[...])
        return carry

    def feed_forward(nf, act, dinner, win, wback, w_sem):
        def fetch(step):
            slot = step % 2
            copies = []
            for f in range(8):
                at = f * (FF // 8) + step * TILE
                into = pl.ds(f * TILE, TILE)
                copies.append(pltpu.make_async_copy(w_in.at[:, pl.ds(at, TILE)], win.at[slot, :, into], w_sem.at[slot, 0, f]))
                copies.append(pltpu.make_async_copy(w_back.at[pl.ds(at, TILE)], wback.at[slot, into], w_sem.at[slot, 1, f]))
            for copy in copies:
                copy.start()
            return copies

        fetched = [fetch(0), fetch(1)]
        wo_copy.wait()
        lax.fori_loop(0, 4, project_out, 0)

        def norm(at, carry):
            blk, half = at // 2, at % 2
            rows = pl.ds(pl.multiple_of(half * 256, 256), 256)
            h = hidden[blk, rows, :]
            r = lax.rsqrt(jnp.mean(h * h, axis=-1, keepdims=True) + EPSILON)
            nf[blk, rows, :] = (h * r * gain_f[...].reshape(1, D)).astype(bf16)
            return carry

        lax.fori_loop(0, 4, norm, 0)
        c_own[0].wait()
        for copy in cot_moves[0]:
            copy.wait_recv()

        for step in range(STEPS):
            slot = step % 2
            for copy in fetched[step]:
                copy.wait()

            def rows_of(at, carry):
                blk, half = at // 2, at % 2
                rows = pl.ds(pl.multiple_of(half * 256, 256), 256)
                within("rows" + str(step), at, 0, 4)
                if step == 0:

                    @pl.when(at == 2)
                    def _():
                        c_own[1].wait()
                        for copy in cot_moves[1]:
                            copy.wait()

                v = nn(nf[blk, rows, :], win[slot])
                square = v * v
                t = jnp.tanh(GELU_A * v * (1.0 + GELU_B * square))
                a = (0.5 * v * (1.0 + t)).astype(bf16)
                slope = 0.5 * (1.0 + t) + 0.5 * GELU_A * v * (1.0 - t * t) * (1.0 + 3.0 * GELU_B * square)
                act[blk, rows, :] = a
                g = (nt(cots[blk, rows, :], wback[slot]) * slope).astype(bf16)
                dinner[blk, rows, :] = g
                onward = nn(a, wback[slot])
                backward = nt(g, win[slot])
                if step == 0:
                    total[blk, rows, :] = hidden[blk, rows, :] + onward
                    back[blk, rows, :] = backward
                else:
                    total[blk, rows, :] += onward
                    back[blk, rows, :] += backward
                return carry

            lax.fori_loop(0, 4, rows_of, 0)
            point("mid" + str(step) + ".0")
            if step + 2 < STEPS:
                fetched.append(fetch(step + 2))
            for b in range(2):
                if b == 1:
                    point("mid" + str(step) + ".b")
                res = tn(flat(nf), flat(dinner, slice(512 * b, 512 * b + 512))).astype(bf16)
                for m in range(4):
                    own[ffn_base(step, 0) + m, :, :, :, b] = res[:, TILE * m : TILE * m + TILE].reshape(2, 2, 2, 96, TILE)
            point("mid" + str(step) + ".1")
            for b in range(2):
                if b == 1:
                    point("mid" + str(step) + ".c")
                res = tn(flat(cots, slice(384 * b, 384 * b + 384)), flat(act)).astype(bf16)
                for m in range(4):
                    for f in range(8):
                        own[ffn_base(step, 1) + m, f // 4, (f // 2) % 2, f % 2, b] = res[
                            96 * m : 96 * m + 96, TILE * f : TILE * f + TILE
                        ]
            point("ffn" + str(step))

    pl.run_scoped(
        feed_forward,
        nf=pltpu.VMEM((OWN, BLOCK, D), bf16),
        act=pltpu.VMEM((OWN, BLOCK, 1024), bf16),
        dinner=pltpu.VMEM((OWN, BLOCK, 1024), bf16),
        win=pltpu.VMEM((2, D, 1024), bf16),
        wback=pltpu.VMEM((2, 1024, D), bf16),
        w_sem=DMA((2, 2, 8)),
    )

    small[0] = jnp.zeros((32, TILE), f32)
    buckets_acc[...] = jnp.zeros_like(buckets_acc)

    def attention_gradients(qs, ks, vs, ps, dsb, acc, far_acc, wq, wk, wv, l_sem, p_sem):
        more = []
        for at, (src, dst) in enumerate(((q_kept, qs), (k_kept, ks), (v_kept, vs), (w_q, wq), (w_k, wk), (w_v, wv))):
            copy = pltpu.make_async_copy(src, dst, l_sem.at[at])
            copy.start()
            more.append(copy)

        def pair_of(at):
            return at // 2 + 3 * (at % 2)

        def probs_copy(n):
            blk, at = n // PAIRS, n % PAIRS
            return pltpu.make_async_copy(p_kept.at[blk * PAIRS + pair_of(at)], ps.at[n % 2], p_sem.at[n % 2])

        probs_copy(0).start()

        which = lax.broadcasted_iota(jnp.int32, (2 * HEADS, D), 0) % HEADS
        spread = (lax.broadcasted_iota(jnp.int32, (2 * HEADS, D), 1) // 64 == which).astype(bf16)

        def close(at, gains):
            blk, half = at // 2, at % 2
            rows = pl.ds(pl.multiple_of(half * 256, 256), 256)
            within("close", at, 0, 4)
            h = hidden[blk, rows, :]
            r = lax.rsqrt(jnp.mean(h * h, axis=-1, keepdims=True) + EPSILON)
            d = back[blk, rows, :]
            scaled = gain_f[...].reshape(1, D) * d
            inner = jnp.mean(h * scaled, axis=-1, keepdims=True)
            grad = cots[blk, rows, :].astype(f32) + r * scaled - h * (r * r * r * inner)
            cots[blk, rows, :] = total[blk, rows, :].astype(bf16)
            hidden[blk, rows, :] = grad
            low_grad = grad.astype(bf16)
            scale = invs[blk, :, 0:2, rows].reshape(HEADS, 256).T
            coarse = scale.astype(bf16)
            scale = jnp.concatenate([coarse, (scale - coarse.astype(f32)).astype(bf16)], axis=1)
            passed = nt(low_grad, wo[...]).astype(bf16)
            dcs[blk, rows, :] = (passed.astype(f32) * nn(scale, spread)).astype(bf16)
            return gains + jnp.sum(d * h * r, axis=0, keepdims=True)

        gains = lax.fori_loop(0, 4, close, jnp.zeros((1, D), f32))
        for m in range(6):
            small[0, 22 + m : 23 + m, :] = gains[:, TILE * m : TILE * m + TILE]
        for blk in range(OWN):
            send_back(cots, output, blk, 0, (3,))[0].start()
        point("closed")
        for copy in more:
            copy.wait()

        lane = lax.broadcasted_iota(jnp.int32, (1, TILE), 1)
        is_low = lane < 64
        first_lane, second_lane = (lane % 64 == 0).astype(bf16), (lane % 64 == 1).astype(bf16)
        source = lax.broadcasted_iota(jnp.int32, (2 * TILE, TILE), 0) // 64 % 2
        swap = (source != lax.broadcasted_iota(jnp.int32, (2 * TILE, TILE), 1) // 64).astype(bf16)
        corner = lax.broadcasted_iota(jnp.int32, (TILE, TILE), 0) + lax.broadcasted_iota(jnp.int32, (TILE, TILE), 1)
        flip = (corner == TILE - 1).astype(bf16)

        def split(value):
            coarse = value.astype(bf16)
            return coarse, (value - coarse.astype(f32)).astype(bf16)

        def attention_back(blk, order, start):
            n = blk * PAIRS + order
            pair = pair_of(order)
            slot = n % 2
            probs_copy(n).wait()

            @pl.when(n + 1 < OWN * PAIRS)
            def _():
                probs_copy(n + 1).start()

            lanes = pl.ds(pl.multiple_of(pair * TILE, TILE), TILE)
            q, k, v, dc = qs[blk, :, lanes], ks[blk, :, lanes], vs[blk, :, lanes], dcs[blk, :, lanes]
            product = dc.astype(f32) * cs[blk, :, lanes].astype(f32)
            delta = nn(jnp.concatenate(split(product), axis=1), swap)
            coarse, fine = split(delta)
            delta = -(coarse * first_lane + fine * second_lane)
            left = (v * low + high, v * high + low)
            right = (dc * low + delta * high, dc * high + delta * low)
            grads = [nt(left[e], right[e]) for e in range(2)]
            found = [None, None]

            def scores_back(e):
                sums = {}
                for qt in range(4):
                    at_q = slice(TILE * qt, TILE * qt + TILE)
                    for kt in range(4):
                        at_k = slice(TILE * kt, TILE * kt + TILE)
                        ds = ps[slot, e, at_k, at_q].astype(f32) * grads[e][at_k, at_q]
                        dsb[e, at_k, at_q] = ds.astype(bf16)
                        sums.setdefault(min(max(kt - qt, -2), 2) + 2, []).append(ds)
                for kind, tiles in sums.items():
                    total_tile = tiles[0]
                    for tile in tiles[1:]:
                        total_tile = total_tile + tile
                    if kind in (0, 4):
                        total_tile = jnp.sum(total_tile.reshape(16, 8, TILE), axis=0)
                        at = (2 * pair + e, kind // 4)
                        far_acc[at] = total_tile if start else far_acc[at] + total_tile
                    else:
                        at = (2 * pair + e, kind - 1)
                        acc[at] = total_tile if start else acc[at] + total_tile

            def products(e):
                rows = slice(64 * e, 64 * e + 64)
                found[e] = (nn(k.T[rows], dsb[e]), nn(dsb[e], q), nn(ps[slot, e], dc))

            scores_back(0)
            products(0)
            scores_back(1)
            products(1)
            qs[blk, :, lanes] = jnp.concatenate([found[0][0], found[1][0]], axis=0).astype(bf16).T
            ks[blk, :, lanes] = jnp.where(is_low, found[0][1], found[1][1]).astype(bf16)
            vs[blk, :, lanes] = jnp.where(is_low, found[0][2], found[1][2]).astype(bf16)

        def first_norm(at, gains):
            blk, half = at // 2, at % 2
            rows = pl.ds(pl.multiple_of(half * 256, 256), 256)
            within("norm0", at, 0, 2)
            within("norm1", at - 2, 0, 2)
            d = nt(qs[blk, rows, :], wq[...]) + nt(ks[blk, rows, :], wk[...]) + nt(vs[blk, rows, :], wv[...])
            h = xs[blk, rows, :].astype(f32)
            r = lax.rsqrt(jnp.mean(h * h, axis=-1, keepdims=True) + EPSILON)
            scaled = gain_a[...].reshape(1, D) * d
            inner = jnp.mean(h * scaled, axis=-1, keepdims=True)
            xs[blk, rows, :] = (hidden[blk, rows, :] + r * scaled - h * (r * r * r * inner)).astype(bf16)
            return gains + jnp.sum(d * h * r, axis=0, keepdims=True)

        def first_block(order, carry):
            within("first", order, 0, PAIRS)
            attention_back(0, order, True)
            return carry

        lax.fori_loop(0, PAIRS, first_block, 0)
        gains = lax.fori_loop(0, 2, first_norm, jnp.zeros((1, D), f32))
        start_back(xs, grad_tokens, 0, 1)
        point("GT0")

        for group in range(3):
            def second_block(order, carry):
                within("second" + str(group), order - 2 * group, 0, 2)
                attention_back(1, order, False)
                return carry

            lax.fori_loop(2 * group, 2 * group + 2, second_block, 0)
            point("second" + str(group) + ".2")
            for side in range(2):
                if side == 1:
                    point("side" + str(group))
                pair = group + 3 * side
                lanes = slice(TILE * pair, TILE * pair + TILE)
                qk = tn(flat(ns), jnp.concatenate([flat(t, lanes) for t in (qs, ks)], axis=1)).astype(bf16)
                grad_v = tn(flat(ns), flat(vs, lanes)).astype(bf16)
                grad_o = tn(flat(cs), flat(hidden, lanes).astype(bf16)).astype(bf16)
                pieces = ((qk[:, :TILE], qk[:, TILE:]), (grad_v, grad_o))
                base = ffn_base(group, 1 - c)
                for kind in range(2):
                    for half in range(2):
                        own[base + 2 * half + kind, :, :, :, side] = pieces[kind][half].reshape(2, 2, 2, 96, TILE)
            point("group" + str(group))

        def diagonals(head, carry):
            sums = []
            for tile in range(3):
                turned = nn(flip, jnp.concatenate(split(acc[head, tile]), axis=1))
                turned = turned[:, :TILE] + turned[:, TILE:]
                wide = jnp.concatenate([turned, jnp.zeros((TILE, TILE), f32)], axis=1)
                wide = pltpu.roll(wide, 0, 1, stride=1, stride_axis=0)
                sums.append(jnp.sum(wide, axis=0, keepdims=True))
            for kind in range(2):
                sums.append(jnp.sum(far_acc[head, kind], axis=0, keepdims=True))
            buckets_acc[pl.ds(head, 1), :] = jnp.concatenate(sums, axis=1)
            return carry

        gains = lax.fori_loop(2, 4, first_norm, gains)
        start_back(xs, grad_tokens, 1, 1)
        point("normed")
        lax.fori_loop(0, HEADS, diagonals, 0)
        for m in range(6):
            small[0, 16 + m : 17 + m, :] = gains[:, TILE * m : TILE * m + TILE]

    pl.run_scoped(
        attention_gradients,
        qs=pltpu.VMEM((OWN, BLOCK, D), bf16),
        ks=pltpu.VMEM((OWN, BLOCK, D), bf16),
        vs=pltpu.VMEM((OWN, BLOCK, D), bf16),
        ps=pltpu.VMEM((2, 2, BLOCK, BLOCK), bf16),
        dsb=pltpu.VMEM((2, BLOCK, BLOCK), bf16),
        acc=pltpu.VMEM((HEADS, 3, TILE, TILE), f32),
        far_acc=pltpu.VMEM((HEADS, 2, 8, TILE), f32),
        wq=pltpu.VMEM((D, D), bf16),
        wk=pltpu.VMEM((D, D), bf16),
        wv=pltpu.VMEM((D, D), bf16),
        l_sem=DMA((6,)),
        p_sem=DMA((2,)),
    )

    lane = lax.broadcasted_iota(jnp.int32, (1, 2 * TILE), 1)
    offsets = jnp.concatenate([TILE * tile + TILE - 1 - lane for tile in (-1, 0, 1)], axis=1)
    far = lax.broadcasted_iota(jnp.int32, (1, 256), 1)
    column = jnp.concatenate([bucket_of(offsets), jnp.where(far < TILE, 15, 31)], axis=1)
    hot = (lax.broadcasted_iota(jnp.int32, (TILE, 1024), 0) == column).astype(f32)
    small[0, 0:16, :] = lax.dot_general(
        buckets_acc[...], hot, (((1,), (1,)), ((), ())), preferred_element_type=f32, precision=lax.Precision.HIGHEST
    )
    copies = [
        remote(small.at[0], small_in.at[at], sm_send.at[at], sm_recv.at[at], {"head": peers[at]}) for at in range(3)
    ]
    for copy in copies:
        copy.start()
    point("small0")
    for copy in copies:
        copy.wait()
    small[1] = (small[0] + small_in[0]) + (small_in[1] + small_in[2])
    copies = [
        remote(small.at[1], small_far.at[at], sm_send.at[3 + at], sm_recv.at[3 + at], column_peers[at]) for at in range(7)
    ]
    for copy in copies:
        copy.start()
    point("small1")
    for copy in copies:
        copy.wait()
    total_small = small[1]
    for at in range(7):
        total_small = total_small + small_far[at]
    g_small[...] = total_small
    point("last")
    assert sorted(set(taken)) == [(item, step) for item in range(6) for step in range(1, 8)]
    wait_back(cots, output, 0)
    wait_back(xs, grad_tokens, 1)
    emit(c, f_ffn, rf_ffn, f_att, rf_att, (g_q, g_k, g_v, g_o), g_in, g_back)


def emit(c, f_ffn, rf_ffn, f_att, rf_att, g_square, g_in, g_back):
    first = c == 0
    for step in range(STEPS):
        for b in range(2):
            kept, got = f_ffn[step, c, b].astype(f32), rf_ffn[step, b].astype(f32)
            g_in[:, 384 * b + TILE * step : 384 * b + TILE * step + TILE] = jnp.where(first, kept, got)
            g_back[96 * b : 96 * b + 96, TILE * step : TILE * step + TILE] = jnp.where(first, got, kept)
    for half in range(2):
        for kind in range(2):
            pieces = []
            for g in range(3):
                kept, got = f_att[g, half].astype(f32), rf_att[g, half].astype(f32)
                pieces.append(jnp.where(first, kept, got) if kind == 0 else jnp.where(first, got, kept))
            wide = jnp.concatenate(pieces, axis=1)
            g_square[2 * kind + half][...] = jnp.where(first, wide[:, :192], wide[:, 192:])


def layer_call(outer, tokens, cot, table, buckets, lengths, w_q, w_k, w_v, w_o, w_in, w_back, gain_a, gain_f):
    rows = (OWN, BLOCK, D)
    local = jax.ShapeDtypeStruct((ROWS, TILE, D), bf16)
    square = jax.ShapeDtypeStruct((96, 192), f32)
    kept = jax.ShapeDtypeStruct(rows, bf16)
    halves = (3, 2)
    scratch = [
        pltpu.VMEM(rows, bf16),
        pltpu.VMEM(rows, bf16),
        pltpu.VMEM(rows, bf16),
        pltpu.VMEM(rows, bf16),
        pltpu.VMEM(rows, f32),
        pltpu.VMEM(rows, f32),
        pltpu.VMEM(rows, f32),
        pltpu.VMEM(rows, bf16),
        pltpu.VMEM((D, D), bf16),
        pltpu.VMEM((OWN, PAIRS, 8, BLOCK), f32),
        pltpu.VMEM((8, TILE), f32),
        pltpu.VMEM((GROUP, 8, TILE), f32),
        pltpu.VMEM((24,) + UNIT, bf16),
        pltpu.VMEM((3, 4) + UNIT, bf16),
        pltpu.VMEM((3, 2) + UNIT, bf16),
    ]
    for dims in ((2,), ()):
        for stage in range(4):
            scratch.append(pltpu.VMEM(halves + dims + (2,) * (3 - stage) + UNIT[4:], bf16))
    scratch += [
        pltpu.VMEM((3, 2, 2) + UNIT[4:], bf16),
        pltpu.VMEM((3, 2) + UNIT[4:], bf16),
        pltpu.VMEM((3, 2) + UNIT[4:], bf16),
        pltpu.VMEM((3, 2) + UNIT[4:], bf16),
        pltpu.VMEM((2, 32, TILE), f32),
        pltpu.VMEM((3, 32, TILE), f32),
        pltpu.VMEM((7, 32, TILE), f32),
        pltpu.VMEM((16, 1024), f32),
        DMA((OWN,)), DMA((OWN, 3)), DMA((OWN, 3)),
        DMA((OWN,)), DMA((OWN, 3)), DMA((OWN, 3)),
        DMA((3,)), DMA((3,)), DMA(()),
        DMA((3,)), DMA((3,)), DMA((3, 2)), DMA((3, 2)),
        DMA((6, 2, 4)), DMA((6, 2, 4)), DMA((6,)), DMA((6,)), DMA((10,)), DMA((10,)),
        DMA((2, OWN)), DMA((2, OWN, 3)), DMA((2, OWN, 3)),
    ]
    results = pl.pallas_call(
        functools.partial(layer_kernel, outer),
        out_shape=(
            local,
            local,
            square,
            square,
            square,
            square,
            jax.ShapeDtypeStruct((96, D), f32),
            jax.ShapeDtypeStruct((192, 384), f32),
            jax.ShapeDtypeStruct((32, TILE), f32),
            kept,
            kept,
            kept,
            jax.ShapeDtypeStruct((OWN * PAIRS, 2, BLOCK, BLOCK), bf16),
        ),
        in_specs=[ANY, ANY, VMEM, VMEM, VMEM] + [ANY] * 6 + [VMEM, VMEM],
        out_specs=(ANY, ANY) + (VMEM,) * 7 + (ANY,) * 4,
        scratch_shapes=scratch,
        compiler_params=pltpu.CompilerParams(collective_id=0, has_side_effects=True, vmem_limit_bytes=63 * 2**20),
    )(tokens, cot, table, buckets, lengths, w_q, w_k, w_v, w_o, w_in, w_back, gain_a, gain_f)
    return results[:9]


def settle_kernel(per, *refs):
    sources, small_in, outs, refs = refs[:8], refs[8], refs[9:20], refs[20:]
    held, (small, read, written, small_sem) = refs[:8], refs[8:]
    pieces = [(0, pl.ds(0, 4)), (0, pl.ds(4, 4)), (1, pl.ds(0, 4)), (1, pl.ds(4, 4))]
    pieces += [(at, slice(None)) for at in range(2, 8)]
    reads = [
        pltpu.make_async_copy(sources[at].at[rows], held[at].at[rows], read.at[n]) for n, (at, rows) in enumerate(pieces)
    ]
    writes = [
        pltpu.make_async_copy(held[at].at[rows], outs[at].at[rows], written.at[n]) for n, (at, rows) in enumerate(pieces)
    ]
    small_copy = pltpu.make_async_copy(small_in, small, small_sem)
    small_copy.start()
    for copy in reads:
        copy.start()
    small_copy.wait()
    me = lax.axis_index("head")

    def mine(options):
        value = options[0]
        for at in range(1, GROUP):
            value = jnp.where(me == at, options[at], value)
        return value

    share = D // GROUP
    for at in range(2):
        whole = jnp.concatenate([small[16 + 6 * at + m : 17 + 6 * at + m, :] for m in range(6)], axis=1)
        outs[8 + at][...] = mine([whole[:, share * j : share * j + share] for j in range(GROUP)]).reshape(share)
    rows = mine([small[per * j : per * j + per, :] for j in range(GROUP)])
    outs[10][...] = rows[:, 0:BUCKETS]
    for get, put in zip(reads, writes):
        get.wait()
        put.start()
    for put in writes:
        put.wait()


def settle_call(per, *values):
    large = values[:8]
    return pl.pallas_call(
        functools.partial(settle_kernel, per),
        out_shape=tuple(jax.ShapeDtypeStruct(v.shape, v.dtype) for v in large)
        + (jax.ShapeDtypeStruct((D // GROUP,), f32),) * 2
        + (jax.ShapeDtypeStruct((per, BUCKETS), f32),),
        in_specs=[ANY] * 9,
        out_specs=(ANY,) * 8 + (VMEM,) * 3,
        scratch_shapes=[pltpu.VMEM(v.shape, v.dtype) for v in values] + [DMA((10,)), DMA((10,)), DMA(())],
        compiler_params=pltpu.CompilerParams(vmem_limit_bytes=63 * 2**20),
    )(*values)


def shards(
    tokens, bucket_of_block, lengths, w_query, w_key, w_value, w_out, w_in, w_back, gain_attn, gain_ffn, bias_table, cotangent
):
    outer = lax.axis_size("dp") // 8
    per = bias_table.shape[1]
    slots = lengths.transpose(0, 2, 1)
    output, grad_tokens, *weights, small = layer_call(
        outer, tokens, cotangent, bias_table.T, bucket_of_block, slots,
        w_query, w_key, w_value, w_out, w_in, w_back, gain_attn, gain_ffn,
    )
    if outer > 1:
        groups = [[at * outer + spare for spare in range(outer)] for at in range(8)]
        weights = [
            lax.psum_scatter(grad, "dp", scatter_dimension=dim, axis_index_groups=groups, tiled=True)
            for grad, dim in zip(weights, (0, 0, 0, 0, 0, 1))
        ]
        small = lax.psum(small, "dp", axis_index_groups=groups)
    results = settle_call(per, output, grad_tokens, *weights, small)
    return results[:7] + (results[7].T,) + results[8:10] + (results[10].T,)


def solution(mesh):
    whole = P()
    rows = P("dp", "head", None)
    block = P("dp", "head")
    return jax.shard_map(
        shards,
        mesh=mesh,
        in_specs=(rows, P("dp", None), P("dp", None, None)) + (whole,) * 8 + (P(None, "head"), rows),
        out_specs=(rows, rows) + (block,) * 6 + (P("head"), P("head"), P(None, "head")),
        check_vma=False,
    )
```

```python
import functools
import math

import jax
import jax.numpy as jnp
from jax import lax
from jax.experimental import pallas as pl
from jax.experimental.pallas import tpu as pltpu
from jax.sharding import PartitionSpec as P

D = 768
HEADS = 12
FF = 3072
BUCKETS = 32
BLOCK = 512
PAIRS = 6
OWN = 2
GROUP = 4
ROWS = 8
EPSILON = 1e-06
TILE = 128
MASKED = -float(2**30)
GELU_A = math.sqrt(2.0 / math.pi)
GELU_B = 0.044715

bf16 = jnp.bfloat16
f32 = jnp.float32
MESH = pl.DeviceIdType.MESH
ANY = pl.BlockSpec(memory_space=pl.ANY)
VMEM = pl.BlockSpec(memory_space=pltpu.VMEM)
DMA = pltpu.SemaphoreType.DMA
STEPS = 3


def nn(left, right):
    return jnp.dot(left, right, preferred_element_type=f32)


def nt(left, right):
    return lax.dot_general(left, right, (((1,), (1,)), ((), ())), preferred_element_type=f32)


def tn(left, right):
    return lax.dot_general(left, right, (((0,), (0,)), ((), ())), preferred_element_type=f32)


def flat(ref, lanes=slice(None)):
    value = ref[:, :, lanes]
    return value.reshape(value.shape[0] * value.shape[1], value.shape[2])


def head_masks():
    lane = lax.broadcasted_iota(jnp.int32, (1, TILE), 1)
    low = (lane < TILE // 2).astype(f32)
    return low.astype(bf16), (1.0 - low).astype(bf16)


def bucket_of(offset):
    magnitude = jnp.abs(offset)
    far = jnp.full(offset.shape, 8, jnp.int32)
    for threshold in (12, 16, 23, 32, 46, 64, 91):
        far = far + (magnitude >= threshold).astype(jnp.int32)
    side = jnp.where(offset > 0, 16, 0).astype(jnp.int32)
    return side + jnp.where(magnitude < 8, magnitude, far)


def skew_offsets(tile):
    lane = lax.broadcasted_iota(jnp.int32, (1, 2 * TILE), 1)
    return TILE * tile + jnp.where(lane < TILE, -lane, 2 * TILE - lane)


ORDERS = (
    (("x", "z0", "z1", "y"), ("z0", "y", "x", "z1")),
    (("x", "z0", "z1", "y"), ("y", "x", "z0", "z1")),
    (("x", "z0", "z1", "y"), ("z0", "x", "y", "z1")),
    (("x", "z0", "z1", "y"), ("z0", "x", "y", "z1")),
    (("x", "y", "z0", "z1"), ("z0", "x", "y", "z1")),
    (("x", "z0", "z1", "y"), ("z0", "x", "y", "z1")),
)
UNIT = (2, 2, 2, 2, 96, TILE)
SLOTS = 4

PLAN = {
    "ffn0": [(0, 1)],
    "rows1.3": [(0, 2)],
    "ffn1": [(1, 1)],
    "rows2.3": [(0, 3), (1, 2)],
    "ffn2": [(2, 1)],
    "close.2": [(0, 4)],
    "closed": [("out", 0)],
    "first.1": [("out", 1), (2, 2)],
    "first.2": [("out", 2)],
    "first.3": [("out", 3)],
    "first.4": [("out", 4), (0, 5), (1, 3)],
    "first.5": [("out", 5)],
    "second0.1": [(2, 3)],
    "group0": [(1, 4), (3, 1)],
    "second1.2": [(0, 6)],
    "side1": [(2, 4), (3, 2)],
    "group1": [(0, 7), (4, 1)],
    "second2.2": [(1, 5)],
    "side2": [(4, 2)],
    "group2": [(5, 1)],
    "normed": [(3, 3)],
    "small0": [(1, 6), (2, 5), (5, 2)],
    "small1": [(1, 7), (3, 4), (4, 3)],
    "last": [(5, 3), (2, 6), (3, 5), (2, 7), (4, 4), (5, 4), (3, 6), (4, 5), (3, 7), (5, 5), (4, 6), (5, 6), (4, 7), (5, 7)],
}


def layer_kernel(
    outer,
    tokens, cot, table, buckets, lengths, w_q, w_k, w_v, w_o, w_in, w_back, gain_a, gain_f,
    output, grad_tokens, g_q, g_k, g_v, g_o, g_in, g_back, g_small, q_kept, k_kept, v_kept, p_kept,
    xs, cots, ns, cs, hidden, total, back, dcs, wo, invs, tab, tabs, own,
    c_ffn, c_att, r0_ffn, r1_ffn, r2_ffn, r3_ffn, r0_att, r1_att, r2_att, r3_att,
    f_ffn, f_att, rf_ffn, rf_att, small, small_in, small_far, buckets_acc,
    own_sem, send_sem, recv_sem, cot_own, cot_send, cot_recv, tab_send, tab_recv, wo_sem,
    cs_send, cs_recv, ca_send, ca_recv, st_send, st_recv, fx_send, fx_recv, sm_send, sm_recv,
    out_own, out_send, out_recv,
):
    me = lax.axis_index("head")
    dp = lax.axis_index("dp")
    y, c = me // 2, me % 2
    chunk, spare = dp // outer, dp % outer
    z1, z0, x = chunk // 4, (chunk // 2) % 2, chunk % 2
    place = {"x": x, "y": y, "z0": z0, "z1": z1}

    def device(row, column):
        return {"dp": row * outer + spare, "head": column}

    partner = {
        "c": device(chunk, 2 * y + (1 - c)),
        "y": device(chunk, 2 * (1 - y) + c),
        "x": device(chunk + 1 - 2 * x, me),
        "z0": device(chunk + 2 - 4 * z0, me),
        "z1": device(chunk + 4 - 8 * z1, me),
    }
    peers = ((1 - y) * 2 + c, (1 - y) * 2 + (1 - c), y * 2 + (1 - c))
    column_peers = [device((chunk + at) % 8, me) for at in range(1, 8)]
    greeted = [{"head": peer} for peer in peers] + column_peers
    barrier = pltpu.get_barrier_semaphore()
    for other in greeted:
        pl.semaphore_signal(barrier, inc=1, device_id=other, device_id_type=MESH)

    def remote(src, dst, sends, recvs, other):
        return pltpu.make_async_remote_copy(
            src_ref=src, dst_ref=dst, send_sem=sends, recv_sem=recvs, device_id=other, device_id_type=MESH
        )

    def mine(start):
        return pl.ds(pl.multiple_of(start * TILE, TILE), TILE)

    x_own = [pltpu.make_async_copy(tokens.at[me + GROUP * blk], xs.at[blk, mine(me)], own_sem.at[blk]) for blk in range(OWN)]
    c_own = [pltpu.make_async_copy(cot.at[me + GROUP * blk], cots.at[blk, mine(me)], cot_own.at[blk]) for blk in range(OWN)]
    wo_copy = pltpu.make_async_copy(w_o, wo, wo_sem)
    for copy in x_own:
        copy.start()
    tab[...] = jnp.zeros_like(tab)
    tab[0 : table.shape[0], 0:BUCKETS] = table[...]
    tabs[me] = tab[...]
    pl.semaphore_wait(barrier, len(greeted))

    def send(source, dest, sends, recvs, blk, at):
        return remote(
            source.at[peers[at] + GROUP * blk], dest.at[blk, mine(me)], sends.at[blk, at], recvs.at[blk, at], {"head": peers[at]}
        )

    moves = [[send(tokens, xs, send_sem, recv_sem, blk, at) for at in range(3)] for blk in range(OWN)]
    cot_moves = [[send(cot, cots, cot_send, cot_recv, blk, at) for at in range(3)] for blk in range(OWN)]
    tab_moves = [remote(tab, tabs.at[me], tab_send.at[at], tab_recv.at[at], {"head": peers[at]}) for at in range(3)]
    for copy in tab_moves:
        copy.start()
    for copy in moves[0]:
        copy.start()

    low, high = head_masks()

    def attention(qs, ks, vs, ps, wq, wk, wv, tiles, marks, w_sem, keep_sem, p_sem):
        weights = [
            pltpu.make_async_copy(src, dst, w_sem.at[at])
            for at, (src, dst) in enumerate(((w_q, wq), (w_k, wk), (w_v, wv)))
        ]
        for copy in weights:
            copy.start()
        for copy in c_own:
            copy.start()
        wo_copy.start()

        def project(blk, half):
            rows = pl.ds(pl.multiple_of(half * 256, 256), 256)
            x = xs[blk, rows, :].astype(f32)
            r = lax.rsqrt(jnp.mean(x * x, axis=-1, keepdims=True) + EPSILON)
            normed = (x * r * gain_a[...].reshape(1, D)).astype(bf16)
            ns[blk, rows, :] = normed
            qs[blk, rows, :] = nn(normed, wq[...]).astype(bf16)
            ks[blk, rows, :] = nn(normed, wk[...]).astype(bf16)
            vs[blk, rows, :] = nn(normed, wv[...]).astype(bf16)

        row = lax.broadcasted_iota(jnp.int32, (BLOCK, TILE), 0).astype(f32)
        column = lax.broadcasted_iota(jnp.int32, (1, TILE), 1) % 64
        document = (column % 4).astype(f32)
        for blk in range(OWN):
            block = me + GROUP * blk
            here = lax.broadcasted_iota(jnp.int32, buckets.shape, 1) == block
            bucket = jnp.sum(jnp.where(here, buckets[...].astype(f32), 0.0), axis=1, keepdims=True)
            span = TILE * jnp.where(bucket == 0.0, 1.0, jnp.where(bucket == 1.0, 2.0, 4.0))
            slots = lengths[0].astype(f32)
            here = lax.broadcasted_iota(jnp.int32, slots.shape, 1) == block
            slots = jnp.sum(jnp.where(here, slots, 0.0), axis=1, keepdims=True)
            real = jnp.zeros((1, TILE), f32)
            for slot in range(4):
                real = jnp.where(document == slot, slots[slot : slot + 1], real)
            start = document * span
            inside = (row >= start) & (row < start + span)
            live = inside & (row < start + real)
            dead = inside & (row >= start + real)
            marks[blk, 0] = jnp.where(column < 4, live.astype(f32), jnp.where(column < 8, dead.astype(f32), 0.0)).astype(bf16)
            marks[blk, 1] = jnp.where(
                column < 4, jnp.where(inside, 0.0, MASKED), jnp.where(column < 8, MASKED, 0.0)
            ).astype(bf16)

        for copy in tab_moves:
            copy.wait()
        bucket_rows = [bucket_of(skew_offsets(tile)) for tile in (-1, 0, 1)]
        for group in range(GROUP):
            rows = tabs[group]
            for tile in range(3):
                values = jnp.zeros((8, 2 * TILE), f32)
                for bucket in range(BUCKETS):
                    values = jnp.where(bucket_rows[tile] == bucket, rows[:, bucket : bucket + 1], values)
                for at in range(3):
                    wide = jnp.broadcast_to(values[at : at + 1], (TILE, 2 * TILE))
                    wide = pltpu.roll(wide, 0, 1, stride=1, stride_axis=0)
                    tiles[3 * group + at, 1 + tile] = wide[:, :TILE]
            for at in range(3):
                tiles[3 * group + at, 0] = jnp.broadcast_to(rows[at : at + 1, 15:16], (TILE, TILE))
                tiles[3 * group + at, 4] = jnp.broadcast_to(rows[at : at + 1, 31:32], (TILE, TILE))

        for copy in weights:
            copy.wait()
        for blk in range(OWN):
            x_own[blk].wait()
        moves[0][2].wait()
        project(0, y)
        for copy in moves[0][:2]:
            copy.wait_send()
        for copy in moves[1]:
            copy.start()
        moves[1][2].wait_recv()
        project(1, y)

        kept = []
        for blk in range(OWN):
            for at, (src, dst) in enumerate(((qs, q_kept), (ks, k_kept), (vs, v_kept))):
                kept.append(pltpu.make_async_copy(src.at[blk], dst.at[blk], keep_sem.at[blk, at]))

        def probs_copy(n):
            return pltpu.make_async_copy(ps.at[n % SLOTS], p_kept.at[n], p_sem.at[n % SLOTS])

        for blk in range(OWN):
            for at in range(2):
                moves[blk][at].wait_recv()
            project(blk, 1 - y)
            for copy in kept[3 * blk : 3 * blk + 3]:
                copy.start()

            def attend(pair, carry):
                n = blk * PAIRS + pair

                @pl.when(pair == 3)
                def _():
                    for copy in (moves[1], cot_moves[0])[blk]:
                        copy.wait_send()
                    for copy in cot_moves[blk]:
                        copy.start()

                slot = n % SLOTS

                @pl.when(n >= SLOTS)
                def _():
                    probs_copy(n - SLOTS).wait()

                lanes = pl.ds(pl.multiple_of(pair * TILE, TILE), TILE)
                q, k, v = qs[blk, :, lanes], ks[blk, :, lanes], vs[blk, :, lanes]
                seen, sees = marks[blk, 0], marks[blk, 1]
                keys = (k * low + seen * high, k * high + seen * low)
                queries = (q * low + sees * high, q * high + sees * low)
                values = ((v * low + high).T, (v * high + low).T)
                scores = [None, None]
                parts = [None, None]

                def score(e):
                    scores[e] = nt(keys[e], queries[e])

                def soften(e):
                    head = 2 * pair + e
                    for qt in range(4):
                        at_q = slice(TILE * qt, TILE * qt + TILE)
                        block = []
                        for kt in range(4):
                            kind = min(max(kt - qt, -2), 2) + 2
                            block.append(scores[e][TILE * kt : TILE * kt + TILE, at_q] + tiles[head, kind])
                        peak = jnp.maximum(jnp.maximum(block[0], block[1]), jnp.maximum(block[2], block[3]))
                        peak = jnp.max(peak, axis=0, keepdims=True)
                        for kt in range(4):
                            ps[slot, e, TILE * kt : TILE * kt + TILE, at_q] = jnp.exp(block[kt] - peak).astype(bf16)

                def gather(e):
                    parts[e] = nn(values[e], ps[slot, e])

                score(0)
                score(1)
                soften(0)
                gather(0)
                soften(1)
                gather(1)
                scale = (1.0 / parts[0][64:65], 1.0 / parts[1][0:1])
                found = jnp.concatenate([parts[0][:64] * scale[0], parts[1][64:] * scale[1]], axis=0)
                cs[blk, :, lanes] = found.astype(bf16).T
                for e in range(2):
                    invs[blk, pair, e : e + 1] = scale[e]
                probs_copy(n).start()
                return carry

            lax.fori_loop(0, PAIRS, attend, 0)
        for n in range(OWN * PAIRS - SLOTS, OWN * PAIRS):
            probs_copy(n).wait()
        for copy in kept:
            copy.wait()

    pl.run_scoped(
        attention,
        qs=pltpu.VMEM((OWN, BLOCK, D), bf16),
        ks=pltpu.VMEM((OWN, BLOCK, D), bf16),
        vs=pltpu.VMEM((OWN, BLOCK, D), bf16),
        ps=pltpu.VMEM((SLOTS, 2, BLOCK, BLOCK), bf16),
        wq=pltpu.VMEM((D, D), bf16),
        wk=pltpu.VMEM((D, D), bf16),
        wv=pltpu.VMEM((D, D), bf16),
        tiles=pltpu.VMEM((HEADS, 5, TILE, TILE), f32),
        marks=pltpu.VMEM((OWN, 2, BLOCK, TILE), bf16),
        w_sem=DMA((3,)),
        keep_sem=DMA((OWN, 3)),
        p_sem=DMA((SLOTS,)),
    )

    def send_back(rows_of, result, at_blk, sems_at, which=(0, 1, 2, 3)):
        copies = []
        for at in which:
            owner = peers[at] if at < 3 else me
            source, target = rows_of.at[at_blk, mine(owner)], result.at[me + GROUP * at_blk]
            if at < 3:
                sems = (out_send.at[sems_at, at_blk, at], out_recv.at[sems_at, at_blk, at])
                copies.append(remote(source, target, *sems, {"head": owner}))
            else:
                copies.append(pltpu.make_async_copy(source, target, out_own.at[sems_at, at_blk]))
        return copies

    def start_back(rows_of, result, at_blk, sems_at):
        for copy in send_back(rows_of, result, at_blk, sems_at):
            copy.start()

    def wait_back(rows_of, result, sems_at):
        for blk in range(OWN):
            for copy in send_back(rows_of, result, blk, sems_at):
                copy.wait()

    def ffn_base(item, kind):
        return (item * 2 + kind) * 4

    def core_copies(item):
        if item < STEPS:
            copies = [
                remote(own.at[pl.ds(ffn_base(item, 1 - c), 4)], c_ffn.at[item], cs_send.at[item], cs_recv.at[item], partner["c"])
            ]
        else:
            g = item - STEPS
            copies = [
                remote(
                    own.at[ffn_base(g, 1 - c) + 2 * half + (1 - c)], c_att.at[g, half],
                    ca_send.at[g, half], ca_recv.at[g, half], partner["c"],
                )
                for half in range(2)
            ]
        return copies

    def add_into(target, arrived):
        target[...] = target[...] + arrived[...]

    def core_finish(item):
        for copy in core_copies(item):
            copy.wait()
        if item < STEPS:
            base = ffn_base(item, c)

            def add(at, carry):
                for b in range(2):
                    add_into(own.at[base + at, b], c_ffn.at[item, at, b])
                return carry

            lax.fori_loop(0, 4, add, 0)
        else:
            g = item - STEPS
            for half in range(2):
                slot = ffn_base(g, 1 - c) + 2 * half + c

                def add(b, carry):
                    add_into(own.at[slot, b], c_att.at[g, half, b])
                    return carry

                lax.fori_loop(0, 2, add, 0)

    def part(item, half, done, axis=None, value=None):
        index = []
        for name in ("z1", "z0", "x", "y"):
            if name == axis:
                index.append(value)
            elif name in done:
                index.append(place[name])
            else:
                index.append(slice(None))
        if item < STEPS:
            lead = pl.ds(ffn_base(item, c) + 2 * half, 2)
        else:
            lead = ffn_base(item - STEPS, 1 - c) + 2 * half + c
        return own.at[tuple([lead] + index)]

    stage_ffn = (r0_ffn, r1_ffn, r2_ffn, r3_ffn)
    stage_att = (r0_att, r1_att, r2_att, r3_att)

    def arrived_at(item, half, stage):
        if item < STEPS:
            return stage_ffn[stage].at[item, half]
        return stage_att[stage].at[item - STEPS, half]

    def stage_copies(item, stage):
        copies = []
        for half in range(2):
            order = ORDERS[item][half]
            axis = order[stage]
            copy = remote(
                part(item, half, order[:stage], axis, 1 - place[axis]), arrived_at(item, half, stage),
                st_send.at[item, half, stage], st_recv.at[item, half, stage], partner[axis],
            )
            copies.append(copy)
        return copies

    def stage_finish(item, stage):
        copies = stage_copies(item, stage)
        for half in range(2):
            copies[half].wait()
            order = ORDERS[item][half]
            kept = part(item, half, order[: stage + 1])
            arrived = arrived_at(item, half, stage)
            if stage < 3:
                add_into(kept, arrived)
            elif item < STEPS:
                f_ffn[item, half] = kept[...] + arrived[...]
            else:
                f_att[item - STEPS, half] = kept[...] + arrived[...]

    def fix_copies(item):
        if item < STEPS:
            copy = remote(f_ffn.at[item, 1 - c], rf_ffn.at[item], fx_send.at[item], fx_recv.at[item], partner["c"])
        else:
            g = item - STEPS
            copy = remote(f_att.at[g], rf_att.at[g], fx_send.at[item], fx_recv.at[item], partner["c"])
        return [copy]

    taken = []

    def advance(item, step):
        taken.append((item, step))
        if step == 2:
            core_finish(item)
        elif 3 <= step < 7:
            stage_finish(item, step - 3)
        if step == 1:
            copies = core_copies(item)
        elif step < 6:
            copies = stage_copies(item, step - 2)
        else:
            copies = fix_copies(item)
        for copy in copies:
            if step == 7:
                copy.wait()
            else:
                copy.start()

    def take(steps):
        for item, step in steps:
            if item == "out":
                send_back(cots, output, step // 3, 0, (step % 3,))[0].start()
            else:
                advance(item, step)

    def point(name):
        take(PLAN.get(name, ()))

    def within(name, at, first, last):
        for value in range(first, last):
            steps = PLAN.get(name + "." + str(value))
            if steps:

                @pl.when(at == value)
                def _():
                    take(steps)

    def project_out(at, carry):
        blk, half = at // 2, at % 2
        rows = pl.ds(pl.multiple_of(half * 256, 256), 256)
        hidden[blk, rows, :] = xs[blk, rows, :].astype(f32) + nn(cs[blk, rows, :], wo[...])
        return carry

    def feed_forward(nf, act, dinner, win, wback, w_sem):
        def fetch(step):
            slot = step % 2
            copies = []
            for f in range(8):
                at = f * (FF // 8) + step * TILE
                into = pl.ds(f * TILE, TILE)
                copies.append(pltpu.make_async_copy(w_in.at[:, pl.ds(at, TILE)], win.at[slot, :, into], w_sem.at[slot, 0, f]))
                copies.append(pltpu.make_async_copy(w_back.at[pl.ds(at, TILE)], wback.at[slot, into], w_sem.at[slot, 1, f]))
            for copy in copies:
                copy.start()
            return copies

        fetched = [fetch(0), fetch(1)]
        wo_copy.wait()
        lax.fori_loop(0, 4, project_out, 0)

        def norm(at, carry):
            blk, half = at // 2, at % 2
            rows = pl.ds(pl.multiple_of(half * 256, 256), 256)
            h = hidden[blk, rows, :]
            r = lax.rsqrt(jnp.mean(h * h, axis=-1, keepdims=True) + EPSILON)
            nf[blk, rows, :] = (h * r * gain_f[...].reshape(1, D)).astype(bf16)
            return carry

        lax.fori_loop(0, 4, norm, 0)
        c_own[0].wait()
        for copy in cot_moves[0]:
            copy.wait_recv()

        for step in range(STEPS):
            slot = step % 2
            for copy in fetched[step]:
                copy.wait()

            def rows_of(at, carry):
                blk, half = at // 2, at % 2
                rows = pl.ds(pl.multiple_of(half * 256, 256), 256)
                within("rows" + str(step), at, 0, 4)
                if step == 0:

                    @pl.when(at == 2)
                    def _():
                        c_own[1].wait()
                        for copy in cot_moves[1]:
                            copy.wait()

                v = nn(nf[blk, rows, :], win[slot])
                square = v * v
                t = jnp.tanh(GELU_A * v * (1.0 + GELU_B * square))
                a = (0.5 * v * (1.0 + t)).astype(bf16)
                slope = 0.5 * (1.0 + t) + 0.5 * GELU_A * v * (1.0 - t * t) * (1.0 + 3.0 * GELU_B * square)
                act[blk, rows, :] = a
                g = (nt(cots[blk, rows, :], wback[slot]) * slope).astype(bf16)
                dinner[blk, rows, :] = g
                onward = nn(a, wback[slot])
                backward = nt(g, win[slot])
                if step == 0:
                    total[blk, rows, :] = hidden[blk, rows, :] + onward
                    back[blk, rows, :] = backward
                else:
                    total[blk, rows, :] += onward
                    back[blk, rows, :] += backward
                return carry

            lax.fori_loop(0, 4, rows_of, 0)
            point("mid" + str(step) + ".0")
            if step + 2 < STEPS:
                fetched.append(fetch(step + 2))
            for b in range(2):
                if b == 1:
                    point("mid" + str(step) + ".b")
                res = tn(flat(nf), flat(dinner, slice(512 * b, 512 * b + 512))).astype(bf16)
                for m in range(4):
                    own[ffn_base(step, 0) + m, :, :, :, b] = res[:, TILE * m : TILE * m + TILE].reshape(2, 2, 2, 96, TILE)
            point("mid" + str(step) + ".1")
            for b in range(2):
                if b == 1:
                    point("mid" + str(step) + ".c")
                res = tn(flat(cots, slice(384 * b, 384 * b + 384)), flat(act)).astype(bf16)
                for m in range(4):
                    for f in range(8):
                        own[ffn_base(step, 1) + m, f // 4, (f // 2) % 2, f % 2, b] = res[
                            96 * m : 96 * m + 96, TILE * f : TILE * f + TILE
                        ]
            point("ffn" + str(step))

    pl.run_scoped(
        feed_forward,
        nf=pltpu.VMEM((OWN, BLOCK, D), bf16),
        act=pltpu.VMEM((OWN, BLOCK, 1024), bf16),
        dinner=pltpu.VMEM((OWN, BLOCK, 1024), bf16),
        win=pltpu.VMEM((2, D, 1024), bf16),
        wback=pltpu.VMEM((2, 1024, D), bf16),
        w_sem=DMA((2, 2, 8)),
    )

    small[0] = jnp.zeros((32, TILE), f32)
    buckets_acc[...] = jnp.zeros_like(buckets_acc)

    def attention_gradients(qs, ks, vs, ps, dsb, acc, far_acc, wq, wk, wv, l_sem, p_sem):
        more = []
        for at, (src, dst) in enumerate(((q_kept, qs), (k_kept, ks), (v_kept, vs), (w_q, wq), (w_k, wk), (w_v, wv))):
            copy = pltpu.make_async_copy(src, dst, l_sem.at[at])
            copy.start()
            more.append(copy)

        def pair_of(at):
            return at // 2 + 3 * (at % 2)

        def probs_copy(n):
            blk, at = n // PAIRS, n % PAIRS
            return pltpu.make_async_copy(p_kept.at[blk * PAIRS + pair_of(at)], ps.at[n % 2], p_sem.at[n % 2])

        probs_copy(0).start()

        which = lax.broadcasted_iota(jnp.int32, (2 * HEADS, D), 0) % HEADS
        spread = (lax.broadcasted_iota(jnp.int32, (2 * HEADS, D), 1) // 64 == which).astype(bf16)

        def close(at, gains):
            blk, half = at // 2, at % 2
            rows = pl.ds(pl.multiple_of(half * 256, 256), 256)
            within("close", at, 0, 4)
            h = hidden[blk, rows, :]
            r = lax.rsqrt(jnp.mean(h * h, axis=-1, keepdims=True) + EPSILON)
            d = back[blk, rows, :]
            scaled = gain_f[...].reshape(1, D) * d
            inner = jnp.mean(h * scaled, axis=-1, keepdims=True)
            grad = cots[blk, rows, :].astype(f32) + r * scaled - h * (r * r * r * inner)
            cots[blk, rows, :] = total[blk, rows, :].astype(bf16)
            hidden[blk, rows, :] = grad
            low_grad = grad.astype(bf16)
            scale = invs[blk, :, 0:2, rows].reshape(HEADS, 256).T
            coarse = scale.astype(bf16)
            scale = jnp.concatenate([coarse, (scale - coarse.astype(f32)).astype(bf16)], axis=1)
            passed = nt(low_grad, wo[...]).astype(bf16)
            dcs[blk, rows, :] = (passed.astype(f32) * nn(scale, spread)).astype(bf16)
            return gains + jnp.sum(d * h * r, axis=0, keepdims=True)

        gains = lax.fori_loop(0, 4, close, jnp.zeros((1, D), f32))
        for m in range(6):
            small[0, 22 + m : 23 + m, :] = gains[:, TILE * m : TILE * m + TILE]
        for blk in range(OWN):
            send_back(cots, output, blk, 0, (3,))[0].start()
        point("closed")
        for copy in more:
            copy.wait()

        lane = lax.broadcasted_iota(jnp.int32, (1, TILE), 1)
        is_low = lane < 64
        first_lane, second_lane = (lane % 64 == 0).astype(bf16), (lane % 64 == 1).astype(bf16)
        source = lax.broadcasted_iota(jnp.int32, (2 * TILE, TILE), 0) // 64 % 2
        swap = (source != lax.broadcasted_iota(jnp.int32, (2 * TILE, TILE), 1) // 64).astype(bf16)
        corner = lax.broadcasted_iota(jnp.int32, (TILE, TILE), 0) + lax.broadcasted_iota(jnp.int32, (TILE, TILE), 1)
        flip = (corner == TILE - 1).astype(bf16)

        def split(value):
            coarse = value.astype(bf16)
            return coarse, (value - coarse.astype(f32)).astype(bf16)

        def attention_back(blk, order, start):
            n = blk * PAIRS + order
            pair = pair_of(order)
            slot = n % 2
            probs_copy(n).wait()

            @pl.when(n + 1 < OWN * PAIRS)
            def _():
                probs_copy(n + 1).start()

            lanes = pl.ds(pl.multiple_of(pair * TILE, TILE), TILE)
            q, k, v, dc = qs[blk, :, lanes], ks[blk, :, lanes], vs[blk, :, lanes], dcs[blk, :, lanes]
            product = dc.astype(f32) * cs[blk, :, lanes].astype(f32)
            delta = nn(jnp.concatenate(split(product), axis=1), swap)
            coarse, fine = split(delta)
            delta = -(coarse * first_lane + fine * second_lane)
            left = (v * low + high, v * high + low)
            right = (dc * low + delta * high, dc * high + delta * low)
            grads = [nt(left[e], right[e]) for e in range(2)]
            found = [None, None]

            def scores_back(e):
                sums = {}
                for qt in range(4):
                    at_q = slice(TILE * qt, TILE * qt + TILE)
                    for kt in range(4):
                        at_k = slice(TILE * kt, TILE * kt + TILE)
                        ds = ps[slot, e, at_k, at_q].astype(f32) * grads[e][at_k, at_q]
                        dsb[e, at_k, at_q] = ds.astype(bf16)
                        sums.setdefault(min(max(kt - qt, -2), 2) + 2, []).append(ds)
                for kind, tiles in sums.items():
                    total_tile = tiles[0]
                    for tile in tiles[1:]:
                        total_tile = total_tile + tile
                    if kind in (0, 4):
                        total_tile = jnp.sum(total_tile.reshape(16, 8, TILE), axis=0)
                        at = (2 * pair + e, kind // 4)
                        far_acc[at] = total_tile if start else far_acc[at] + total_tile
                    else:
                        at = (2 * pair + e, kind - 1)
                        acc[at] = total_tile if start else acc[at] + total_tile

            def products(e):
                rows = slice(64 * e, 64 * e + 64)
                found[e] = (nn(k.T[rows], dsb[e]), nn(dsb[e], q), nn(ps[slot, e], dc))

            scores_back(0)
            products(0)
            scores_back(1)
            products(1)
            qs[blk, :, lanes] = jnp.concatenate([found[0][0], found[1][0]], axis=0).astype(bf16).T
            ks[blk, :, lanes] = jnp.where(is_low, found[0][1], found[1][1]).astype(bf16)
            vs[blk, :, lanes] = jnp.where(is_low, found[0][2], found[1][2]).astype(bf16)

        def first_norm(at, gains):
            blk, half = at // 2, at % 2
            rows = pl.ds(pl.multiple_of(half * 256, 256), 256)
            within("norm0", at, 0, 2)
            within("norm1", at - 2, 0, 2)
            d = nt(qs[blk, rows, :], wq[...]) + nt(ks[blk, rows, :], wk[...]) + nt(vs[blk, rows, :], wv[...])
            h = xs[blk, rows, :].astype(f32)
            r = lax.rsqrt(jnp.mean(h * h, axis=-1, keepdims=True) + EPSILON)
            scaled = gain_a[...].reshape(1, D) * d
            inner = jnp.mean(h * scaled, axis=-1, keepdims=True)
            xs[blk, rows, :] = (hidden[blk, rows, :] + r * scaled - h * (r * r * r * inner)).astype(bf16)
            return gains + jnp.sum(d * h * r, axis=0, keepdims=True)

        def first_block(order, carry):
            within("first", order, 0, PAIRS)
            attention_back(0, order, True)
            return carry

        lax.fori_loop(0, PAIRS, first_block, 0)
        gains = lax.fori_loop(0, 2, first_norm, jnp.zeros((1, D), f32))
        start_back(xs, grad_tokens, 0, 1)
        point("GT0")

        for group in range(3):
            def second_block(order, carry):
                within("second" + str(group), order - 2 * group, 0, 2)
                attention_back(1, order, False)
                return carry

            lax.fori_loop(2 * group, 2 * group + 2, second_block, 0)
            point("second" + str(group) + ".2")
            for side in range(2):
                if side == 1:
                    point("side" + str(group))
                pair = group + 3 * side
                lanes = slice(TILE * pair, TILE * pair + TILE)
                qk = tn(flat(ns), jnp.concatenate([flat(t, lanes) for t in (qs, ks)], axis=1)).astype(bf16)
                grad_v = tn(flat(ns), flat(vs, lanes)).astype(bf16)
                grad_o = tn(flat(cs), flat(hidden, lanes).astype(bf16)).astype(bf16)
                pieces = ((qk[:, :TILE], qk[:, TILE:]), (grad_v, grad_o))
                base = ffn_base(group, 1 - c)
                for kind in range(2):
                    for half in range(2):
                        own[base + 2 * half + kind, :, :, :, side] = pieces[kind][half].reshape(2, 2, 2, 96, TILE)
            point("group" + str(group))

        def diagonals(head, carry):
            sums = []
            for tile in range(3):
                turned = nn(flip, jnp.concatenate(split(acc[head, tile]), axis=1))
                turned = turned[:, :TILE] + turned[:, TILE:]
                wide = jnp.concatenate([turned, jnp.zeros((TILE, TILE), f32)], axis=1)
                wide = pltpu.roll(wide, 0, 1, stride=1, stride_axis=0)
                sums.append(jnp.sum(wide, axis=0, keepdims=True))
            for kind in range(2):
                sums.append(jnp.sum(far_acc[head, kind], axis=0, keepdims=True))
            buckets_acc[pl.ds(head, 1), :] = jnp.concatenate(sums, axis=1)
            return carry

        gains = lax.fori_loop(2, 4, first_norm, gains)
        start_back(xs, grad_tokens, 1, 1)
        point("normed")
        lax.fori_loop(0, HEADS, diagonals, 0)
        for m in range(6):
            small[0, 16 + m : 17 + m, :] = gains[:, TILE * m : TILE * m + TILE]

    pl.run_scoped(
        attention_gradients,
        qs=pltpu.VMEM((OWN, BLOCK, D), bf16),
        ks=pltpu.VMEM((OWN, BLOCK, D), bf16),
        vs=pltpu.VMEM((OWN, BLOCK, D), bf16),
        ps=pltpu.VMEM((2, 2, BLOCK, BLOCK), bf16),
        dsb=pltpu.VMEM((2, BLOCK, BLOCK), bf16),
        acc=pltpu.VMEM((HEADS, 3, TILE, TILE), f32),
        far_acc=pltpu.VMEM((HEADS, 2, 8, TILE), f32),
        wq=pltpu.VMEM((D, D), bf16),
        wk=pltpu.VMEM((D, D), bf16),
        wv=pltpu.VMEM((D, D), bf16),
        l_sem=DMA((6,)),
        p_sem=DMA((2,)),
    )

    lane = lax.broadcasted_iota(jnp.int32, (1, 2 * TILE), 1)
    offsets = jnp.concatenate([TILE * tile + TILE - 1 - lane for tile in (-1, 0, 1)], axis=1)
    far = lax.broadcasted_iota(jnp.int32, (1, 256), 1)
    column = jnp.concatenate([bucket_of(offsets), jnp.where(far < TILE, 15, 31)], axis=1)
    hot = (lax.broadcasted_iota(jnp.int32, (TILE, 1024), 0) == column).astype(f32)
    small[0, 0:16, :] = lax.dot_general(
        buckets_acc[...], hot, (((1,), (1,)), ((), ())), preferred_element_type=f32, precision=lax.Precision.HIGHEST
    )
    copies = [
        remote(small.at[0], small_in.at[at], sm_send.at[at], sm_recv.at[at], {"head": peers[at]}) for at in range(3)
    ]
    for copy in copies:
        copy.start()
    point("small0")
    for copy in copies:
        copy.wait()
    small[1] = (small[0] + small_in[0]) + (small_in[1] + small_in[2])
    copies = [
        remote(small.at[1], small_far.at[at], sm_send.at[3 + at], sm_recv.at[3 + at], column_peers[at]) for at in range(7)
    ]
    for copy in copies:
        copy.start()
    point("small1")
    for copy in copies:
        copy.wait()
    total_small = small[1]
    for at in range(7):
        total_small = total_small + small_far[at]
    g_small[...] = total_small
    point("last")
    assert sorted(set(taken)) == [(item, step) for item in range(6) for step in range(1, 8)]
    wait_back(cots, output, 0)
    wait_back(xs, grad_tokens, 1)
    emit(c, f_ffn, rf_ffn, f_att, rf_att, (g_q, g_k, g_v, g_o), g_in, g_back)


def emit(c, f_ffn, rf_ffn, f_att, rf_att, g_square, g_in, g_back):
    first = c == 0
    for step in range(STEPS):
        for b in range(2):
            kept, got = f_ffn[step, c, b].astype(f32), rf_ffn[step, b].astype(f32)
            g_in[:, 384 * b + TILE * step : 384 * b + TILE * step + TILE] = jnp.where(first, kept, got)
            g_back[96 * b : 96 * b + 96, TILE * step : TILE * step + TILE] = jnp.where(first, got, kept)
    for half in range(2):
        for kind in range(2):
            pieces = []
            for g in range(3):
                kept, got = f_att[g, half].astype(f32), rf_att[g, half].astype(f32)
                pieces.append(jnp.where(first, kept, got) if kind == 0 else jnp.where(first, got, kept))
            wide = jnp.concatenate(pieces, axis=1)
            g_square[2 * kind + half][...] = jnp.where(first, wide[:, :192], wide[:, 192:])


def layer_call(outer, tokens, cot, table, buckets, lengths, w_q, w_k, w_v, w_o, w_in, w_back, gain_a, gain_f):
    rows = (OWN, BLOCK, D)
    local = jax.ShapeDtypeStruct((ROWS, TILE, D), bf16)
    square = jax.ShapeDtypeStruct((96, 192), f32)
    kept = jax.ShapeDtypeStruct(rows, bf16)
    halves = (3, 2)
    scratch = [
        pltpu.VMEM(rows, bf16),
        pltpu.VMEM(rows, bf16),
        pltpu.VMEM(rows, bf16),
        pltpu.VMEM(rows, bf16),
        pltpu.VMEM(rows, f32),
        pltpu.VMEM(rows, f32),
        pltpu.VMEM(rows, f32),
        pltpu.VMEM(rows, bf16),
        pltpu.VMEM((D, D), bf16),
        pltpu.VMEM((OWN, PAIRS, 8, BLOCK), f32),
        pltpu.VMEM((8, TILE), f32),
        pltpu.VMEM((GROUP, 8, TILE), f32),
        pltpu.VMEM((24,) + UNIT, bf16),
        pltpu.VMEM((3, 4) + UNIT, bf16),
        pltpu.VMEM((3, 2) + UNIT, bf16),
    ]
    for dims in ((2,), ()):
        for stage in range(4):
            scratch.append(pltpu.VMEM(halves + dims + (2,) * (3 - stage) + UNIT[4:], bf16))
    scratch += [
        pltpu.VMEM((3, 2, 2) + UNIT[4:], bf16),
        pltpu.VMEM((3, 2) + UNIT[4:], bf16),
        pltpu.VMEM((3, 2) + UNIT[4:], bf16),
        pltpu.VMEM((3, 2) + UNIT[4:], bf16),
        pltpu.VMEM((2, 32, TILE), f32),
        pltpu.VMEM((3, 32, TILE), f32),
        pltpu.VMEM((7, 32, TILE), f32),
        pltpu.VMEM((16, 1024), f32),
        DMA((OWN,)), DMA((OWN, 3)), DMA((OWN, 3)),
        DMA((OWN,)), DMA((OWN, 3)), DMA((OWN, 3)),
        DMA((3,)), DMA((3,)), DMA(()),
        DMA((3,)), DMA((3,)), DMA((3, 2)), DMA((3, 2)),
        DMA((6, 2, 4)), DMA((6, 2, 4)), DMA((6,)), DMA((6,)), DMA((10,)), DMA((10,)),
        DMA((2, OWN)), DMA((2, OWN, 3)), DMA((2, OWN, 3)),
    ]
    results = pl.pallas_call(
        functools.partial(layer_kernel, outer),
        out_shape=(
            local,
            local,
            square,
            square,
            square,
            square,
            jax.ShapeDtypeStruct((96, D), f32),
            jax.ShapeDtypeStruct((192, 384), f32),
            jax.ShapeDtypeStruct((32, TILE), f32),
            kept,
            kept,
            kept,
            jax.ShapeDtypeStruct((OWN * PAIRS, 2, BLOCK, BLOCK), bf16),
        ),
        in_specs=[ANY, ANY, VMEM, VMEM, VMEM] + [ANY] * 6 + [VMEM, VMEM],
        out_specs=(ANY, ANY) + (VMEM,) * 7 + (ANY,) * 4,
        scratch_shapes=scratch,
        compiler_params=pltpu.CompilerParams(collective_id=0, has_side_effects=True, vmem_limit_bytes=63 * 2**20),
    )(tokens, cot, table, buckets, lengths, w_q, w_k, w_v, w_o, w_in, w_back, gain_a, gain_f)
    return results[:9]


def settle_kernel(per, *refs):
    sources, small_in, outs, refs = refs[:8], refs[8], refs[9:20], refs[20:]
    held, (small, read, written, small_sem) = refs[:8], refs[8:]
    pieces = [(0, pl.ds(0, 4)), (0, pl.ds(4, 4)), (1, pl.ds(0, 4)), (1, pl.ds(4, 4))]
    pieces += [(at, slice(None)) for at in range(2, 8)]
    reads = [
        pltpu.make_async_copy(sources[at].at[rows], held[at].at[rows], read.at[n]) for n, (at, rows) in enumerate(pieces)
    ]
    writes = [
        pltpu.make_async_copy(held[at].at[rows], outs[at].at[rows], written.at[n]) for n, (at, rows) in enumerate(pieces)
    ]
    small_copy = pltpu.make_async_copy(small_in, small, small_sem)
    small_copy.start()
    for copy in reads:
        copy.start()
    small_copy.wait()
    me = lax.axis_index("head")

    def mine(options):
        value = options[0]
        for at in range(1, GROUP):
            value = jnp.where(me == at, options[at], value)
        return value

    share = D // GROUP
    for at in range(2):
        whole = jnp.concatenate([small[16 + 6 * at + m : 17 + 6 * at + m, :] for m in range(6)], axis=1)
        outs[8 + at][...] = mine([whole[:, share * j : share * j + share] for j in range(GROUP)]).reshape(share)
    rows = mine([small[per * j : per * j + per, :] for j in range(GROUP)])
    outs[10][...] = rows[:, 0:BUCKETS]
    for get, put in zip(reads, writes):
        get.wait()
        put.start()
    for put in writes:
        put.wait()


def settle_call(per, *values):
    large = values[:8]
    return pl.pallas_call(
        functools.partial(settle_kernel, per),
        out_shape=tuple(jax.ShapeDtypeStruct(v.shape, v.dtype) for v in large)
        + (jax.ShapeDtypeStruct((D // GROUP,), f32),) * 2
        + (jax.ShapeDtypeStruct((per, BUCKETS), f32),),
        in_specs=[ANY] * 9,
        out_specs=(ANY,) * 8 + (VMEM,) * 3,
        scratch_shapes=[pltpu.VMEM(v.shape, v.dtype) for v in values] + [DMA((10,)), DMA((10,)), DMA(())],
        compiler_params=pltpu.CompilerParams(vmem_limit_bytes=63 * 2**20),
    )(*values)


def shards(
    tokens, bucket_of_block, lengths, w_query, w_key, w_value, w_out, w_in, w_back, gain_attn, gain_ffn, bias_table, cotangent
):
    outer = lax.axis_size("dp") // 8
    per = bias_table.shape[1]
    slots = lengths.transpose(0, 2, 1)
    output, grad_tokens, *weights, small = layer_call(
        outer, tokens, cotangent, bias_table.T, bucket_of_block, slots,
        w_query, w_key, w_value, w_out, w_in, w_back, gain_attn, gain_ffn,
    )
    if outer > 1:
        groups = [[at * outer + spare for spare in range(outer)] for at in range(8)]
        weights = [
            lax.psum_scatter(grad, "dp", scatter_dimension=dim, axis_index_groups=groups, tiled=True)
            for grad, dim in zip(weights, (0, 0, 0, 0, 0, 1))
        ]
        small = lax.psum(small, "dp", axis_index_groups=groups)
    results = settle_call(per, output, grad_tokens, *weights, small)
    return results[:7] + (results[7].T,) + results[8:10] + (results[10].T,)


def solution(mesh):
    whole = P()
    rows = P("dp", "head", None)
    block = P("dp", "head")
    return jax.shard_map(
        shards,
        mesh=mesh,
        in_specs=(rows, P("dp", None), P("dp", None, None)) + (whole,) * 8 + (P(None, "head"), rows),
        out_specs=(rows, rows) + (block,) * 6 + (P("head"), P("head"), P(None, "head")),
        check_vma=False,
    )
```
